32 devices in a mesh: groups: 2 (over y), side: 4 (over x, core), tensor: 4 (over z).
Axes of the slice: x: 2, y: 2, z: 4, core: 2. Of those that a mesh axis runs over, the one named last changes fastest.
Arguments:
- query: bfloat16 [128, 6144], P(('groups', 'side'), 'tensor'), parts along dimension 0, may hold values from -160 to 160
- new_key: bfloat16 [128, 1024], P(('groups', 'side'), 'tensor'), parts along dimension 0, may hold values from -6 to 6
- new_value: bfloat16 [128, 1024], P(('groups', 'side'), 'tensor'), parts along dimension 0, may hold values from -6 to 6
- key_cache: bfloat16 [128, 256, 1024], P(('groups', 'side'), None, 'tensor'), parts along dimension 0, may hold values from -6.5 to 6.5
- value_cache: bfloat16 [128, 256, 1024], P(('groups', 'side'), None, 'tensor'), parts along dimension 0, may hold values from -6 to 6
- cache_len: int32 [128], P(('groups', 'side')), parts along dimension 0, may hold values from 2 to 256, as said below
- resid: bfloat16 [128, 6144], P(('groups', 'side')), parts along dimension 0, may hold values from -4 to 4
- w_out: bfloat16 [6144, 6144], P('tensor', 'side'), may hold values from -0.625 to 0.625
- rms_gain: bfloat16 [6144], replicated, may hold values from 0.099609375 to 1.8984375
- w_router: float32 [6144, 8], replicated, may hold values from -0.15625 to 0.15625
- route_ids: int32 [128, 2], P(('groups', 'side')), parts along dimension 0, may hold values from 0 to 7, all different within a row; in each aligned block of 16 rows (0 to 15, 16 to 31, ...) at most 12 rows name the same one
- w_gate: bfloat16 [8, 6144, 8192], P('side', None, 'tensor'), may hold values from -0.078125 to 0.078125
- w_up: bfloat16 [8, 6144, 8192], P('side', None, 'tensor'), may hold values from -0.078125 to 0.078125
- w_down: bfloat16 [8, 8192, 6144], P('side', 'tensor'), may hold values from -0.0625 to 0.0625
Outputs:
- layer_out: bfloat16 [128, 6144], P(('groups', 'side'), 'tensor'), parts along dimension 0
The draws below stay inside these ranges and needn't reach their ends.
There are 2 independent parts, one for each index of `groups`. The reference program is written for one: setup_inputs(seed, part) draws one part's arguments, and reference() takes and returns one part's arrays. A program takes and returns all parts, laid end to end along the dimension named above; an argument that names none is the same for every part. Nothing has to cross between parts.
Inputs may be any that keep to these rules, and one draw needn't show every extreme that they name: `cache_len`: at least one game of each pool has exactly 256 valid positions. `route_ids`: within the games of one index of side (aligned blocks of 16 games), no expert is chosen by more than 12 games, a bound that some block reaches.
All inputs are finite; a program needn't handle non-finite values.
Results may differ from the reference program's by a relative error of at most 0.0095.
Values may be sent and summed in bfloat16 or wider, within the bound.
No kernel may reach another device: no remote copies, remote signals or barrier semaphores. Data moves between devices by JAX's collectives and lax.ppermute only.
A program may use at most 320 MiB of HBM per device.

```python
import math
import jax
import jax.numpy as jnp
import numpy as np
from jax import lax

D = 6144
HEADS = 48
KV_HEADS = 8
HEAD_DIM = 128
EXPERTS = 8
FFW = 8192
CTX = 256
GAMES_DEV = 16
GAMES = 64
CAP = 12
SPLIT = 1
SLOTS = 8
FFP = 8192


def anchor_keys(key):
    noise = jax.random.normal(jax.random.fold_in(key, 101), (GAMES, KV_HEADS * HEAD_DIM), jnp.float32)
    return jnp.clip(noise, -6.0, 6.0)


def draw_query(key, part):
    key = jax.random.fold_in(key, 1)
    first_key = jax.random.fold_in(key, 0)
    values = jnp.clip(jax.random.normal(first_key, (GAMES, HEADS * HEAD_DIM), jnp.float32), -6.0, 6.0)
    return values.astype(jnp.bfloat16)


def draw_key_cache(key, part):
    anchor = anchor_keys(key)
    key = jax.random.fold_in(key, 2)
    first_key = jax.random.fold_in(key, 0)
    values = jnp.clip(jax.random.normal(first_key, (GAMES, CTX, KV_HEADS * HEAD_DIM), jnp.float32), -6.0, 6.0)
    values = values.at[:, 0, :].set(anchor)
    return values.astype(jnp.bfloat16)


def draw_cache_len(key, part):
    key = jax.random.fold_in(key, 3)
    first_key, second_key, third_key, fourth_key = jax.random.split(key, 4)
    first = jax.random.randint(first_key, (GAMES,), 2, CTX + 1)
    second = jax.random.randint(second_key, (GAMES,), 2, CTX + 1)
    coin = jax.random.randint(third_key, (GAMES,), 0, 2) == 0
    lengths = jnp.where(coin, jnp.minimum(first, second), first)
    longest = jax.random.randint(fourth_key, (), 0, GAMES)
    lengths = jnp.where(jnp.arange(GAMES) == longest, CTX, lengths)
    return lengths.astype(jnp.int32)


def shard_levels(key, shape, cuts, smallest, high):
    factor_of = 1.0
    for position, shards_of in cuts:
        draws = jax.random.uniform(jax.random.fold_in(jax.random.fold_in(key, 6), position), (shards_of,), jnp.float32, smallest / len(cuts), high / len(cuts))
        factor_of = factor_of * jnp.repeat(jnp.exp(draws), shape[position] // shards_of).reshape((-1,) + (1,) * (len(shape) - 1 - position))
    return factor_of


def deal_out(stream_key, own, number, rows, count, top, reach, lean):
    order = jax.random.permutation(stream_key, count)
    heavy_load, ordinary = shares(count, rows * top, reach, lean, True), shares(count, rows * top, reach, lean, False)
    places = jnp.arange(count)

    def named(tallies, rotation):
        used = int((tallies > 0).sum())
        fixed = max(1, used // 4)
        moved = fixed + (places - fixed + rotation * (used - fixed)) % max(1, count - fixed)
        return jnp.zeros((count,), jnp.int32).at[order[jnp.where(places < fixed, places, moved)]].set(jnp.asarray(tallies, jnp.int32))

    tallies = jnp.where(number % 4 == 0, named(heavy_load, number // 4), named(ordinary, number - number // 4 - 1))
    mixed = jax.random.permutation(jax.random.fold_in(own, 3), count)
    source_of, sink = mixed[0:count // 2 * 2:2], mixed[1:count // 2 * 2:2]
    margin = jnp.minimum(tallies[source_of] - 1, reach - tallies[sink]) // 2
    margin = jnp.where((source_of == order[0]) | (sink == order[0]) | (tallies[sink] == 0), 0, jnp.maximum(margin, 0))
    moved = jax.random.randint(jax.random.fold_in(own, 4), (count // 2,), 0, 1 << 20) % (margin + 1)
    tallies = tallies.at[source_of].add(-moved).at[sink].add(moved)
    items = jnp.searchsorted(jnp.cumsum(tallies), jnp.arange(rows * top), side="right").astype(jnp.int32)
    table = items.reshape(top, rows).T
    table = table[jax.random.permutation(jax.random.fold_in(own, 1), rows)]
    rotation = jax.random.randint(jax.random.fold_in(own, 2), (rows, 1), 0, top)
    return jnp.take_along_axis(table, (jnp.arange(top)[None, :] + rotation) % top, axis=1)


def shares(number_of, total, limit, slope, full):
    weights = [(1 << 20) // math.isqrt(standing ** slope) + 1 for standing in range(1, number_of + 1)]
    largest = limit if full else min(limit, max(-(-total // number_of), total * weights[0] // sum(weights)))
    least = 1 if total - largest >= number_of - 1 else 0
    counts, spare = [largest] + [least] * (number_of - 1), total - largest - least * (number_of - 1)
    while spare > 0:
        free = [i for i in range(1, number_of) if counts[i] < largest] or [i for i in range(1, number_of) if counts[i] < limit]
        pool, budget = sum([weights[i] for i in free]), spare
        for i in free:
            more = min(limit - counts[i], max(1, budget * weights[i] // pool), spare)
            counts[i] = counts[i] + more
            spare = spare - more
    return np.array(counts)


def gaussian(key, dims, deviation, limit, pieces=(), held_as=jnp.bfloat16):
    gain = shard_levels(key, dims, pieces, -0.22, 0.18) if pieces else 1.0
    result = jax.random.normal(key, dims, jnp.float32) * deviation * gain
    return jnp.minimum(jnp.maximum(result, -limit), limit).astype(held_as)


def setup_inputs(seed: int = 0, part: int = 0) -> dict:
    key_of = jax.random.split(jax.random.key(seed), 15)
    own_keys = jax.random.split(jax.random.fold_in(key_of[14], part), 15)
    query = draw_query(jax.random.fold_in(jax.random.fold_in(key_of[14], part), 71), part)
    new_key = gaussian(own_keys[1], (GAMES, KV_HEADS * HEAD_DIM), 1.0, 6.0, ((0, 4), (1, 4)))
    new_value = gaussian(own_keys[2], (GAMES, KV_HEADS * HEAD_DIM), 1.0, 6.0, ((0, 4), (1, 4)))
    key_cache = draw_key_cache(jax.random.fold_in(jax.random.fold_in(key_of[14], part), 71), part)
    value_cache = gaussian(own_keys[4], (GAMES, CTX, KV_HEADS * HEAD_DIM), 1.0, 6.0, ((0, 4), (2, 4)))
    cache_len = draw_cache_len(jax.random.fold_in(jax.random.fold_in(key_of[14], part), 71), part)
    resid = gaussian(own_keys[6], (GAMES, D), 0.5, 4.0, ((0, 4),))
    w_out = gaussian(key_of[7], (D, D), (D // 64) ** -0.5, 0.625, ((0, 4), (1, 4)))
    rms_gain = jnp.clip(1.0 + 0.18 * jax.random.normal(key_of[8], (D,), jnp.float32), 0.099609375, 1.8984375).astype(jnp.bfloat16)
    w_router = gaussian(key_of[9], (D, EXPERTS), (D // 4) ** -0.5, 0.15625, (), jnp.float32)
    route_ids_keys = jax.random.split(jax.random.fold_in(own_keys[10], 1), GAMES // GAMES_DEV)
    route_ids_turns = jax.random.permutation(jax.random.fold_in(own_keys[10], 3), GAMES // GAMES_DEV)
    route_ids = jax.vmap(lambda own, number: deal_out(jax.random.fold_in(own_keys[10], 2), own, number, GAMES_DEV, EXPERTS, 2, CAP, 2))(route_ids_keys, route_ids_turns).reshape((GAMES, 2))
    w_gate = gaussian(key_of[11], (SLOTS, D, FFP), D ** -0.5, 0.078125, ((0, 4), (2, 4)))
    w_up = gaussian(key_of[12], (SLOTS, D, FFP), D ** -0.5, 0.078125, ((0, 4), (2, 4)))
    w_down = gaussian(key_of[13], (SLOTS, FFP, D), FFW ** -0.5, 0.0625, ((0, 4), (1, 4)))
    return {"query": query, "new_key": new_key, "new_value": new_value, "key_cache": key_cache, "value_cache": value_cache, "cache_len": cache_len, "resid": resid, "w_out": w_out, "rms_gain": rms_gain, "w_router": w_router, "route_ids": route_ids, "w_gate": w_gate, "w_up": w_up, "w_down": w_down}


def attend_all(query, new_key, new_value, key_cache, value_cache, cache_len):
    count = query.shape[0]
    repeat = HEADS // KV_HEADS
    queries = query.astype(jnp.float32).reshape(count, KV_HEADS, repeat, HEAD_DIM)
    cached_keys = key_cache.astype(jnp.float32).reshape(count, CTX, KV_HEADS, HEAD_DIM)
    cached_values = value_cache.astype(jnp.float32).reshape(count, CTX, KV_HEADS, HEAD_DIM)
    scale = 1.0 / HEAD_DIM ** 0.5
    scores = jnp.einsum('gkrd,gpkd->gkrp', queries, cached_keys) * scale
    own_key = new_key.astype(jnp.float32).reshape(count, KV_HEADS, HEAD_DIM)
    own_score = jnp.einsum('gkrd,gkd->gkr', queries, own_key) * scale
    valid = jnp.arange(CTX, dtype=jnp.int32)[None, :] < cache_len[:, None]
    scores = jnp.where(valid[:, None, None, :], scores, -jnp.inf)
    highest = jnp.maximum(lax.optimization_barrier(jnp.max(scores, axis=-1)), own_score)
    cached_weight = jnp.exp(scores - highest[..., None])
    own_weight = jnp.exp(own_score - highest)
    total = lax.optimization_barrier(jnp.sum(cached_weight, axis=-1)) + own_weight
    cached_weight = (cached_weight / total[..., None]).astype(jnp.bfloat16)
    own_weight = (own_weight / total).astype(jnp.bfloat16)
    mixed = jnp.einsum('gkrp,gpkd->gkrd', cached_weight.astype(jnp.float32), cached_values)
    own_value = new_value.astype(jnp.float32).reshape(count, KV_HEADS, 1, HEAD_DIM)
    mixed = mixed + own_weight.astype(jnp.float32)[..., None] * own_value
    return mixed.reshape(count, HEADS * HEAD_DIM).astype(jnp.bfloat16)

def reference(query, new_key, new_value, key_cache, value_cache, cache_len, resid, w_out, rms_gain, w_router, route_ids, w_gate, w_up, w_down):
    attended = attend_all(query, new_key, new_value, key_cache, value_cache, cache_len)
    attn_out = jnp.dot(attended, w_out, preferred_element_type=jnp.float32)
    stream = (resid.astype(jnp.float32) + attn_out).astype(jnp.bfloat16)
    wide = stream.astype(jnp.float32)
    power = lax.optimization_barrier(jnp.mean(wide * wide, axis=-1, keepdims=True))
    normed = wide * lax.rsqrt(power + 1e-05) * rms_gain.astype(jnp.float32)
    logits = jnp.dot(normed, w_router, precision=lax.Precision.HIGHEST)
    picked = route_ids[:, :, None] == jnp.arange(EXPERTS, dtype=jnp.int32)[None, None, :]
    chosen = lax.optimization_barrier(jnp.sum(jnp.where(picked, logits[:, None, :], 0.0), axis=-1))
    first = 1.0 / (1.0 + jnp.exp(chosen[:, 1] - chosen[:, 0]))
    second = 1.0 / (1.0 + jnp.exp(chosen[:, 0] - chosen[:, 1]))
    pair = jnp.stack([first, second], axis=1)
    weight = lax.optimization_barrier(jnp.sum(jnp.where(picked, pair[:, :, None], 0.0), axis=1))
    rows = normed.astype(jnp.bfloat16)

    def add_slot(total, inputs):
        gate_part, up_part, down_part, slot_index = inputs
        gate = jnp.dot(rows, gate_part, preferred_element_type=jnp.float32)
        upward = jnp.dot(rows, up_part, preferred_element_type=jnp.float32)
        inner = (jax.nn.silu(gate) * upward).astype(jnp.bfloat16)
        output = jnp.dot(inner, down_part, preferred_element_type=jnp.float32)
        column = lax.dynamic_slice_in_dim(weight, (slot_index // SPLIT).astype(jnp.int32), 1, 1)
        return (total + column * output, None)
    start = jnp.zeros((rows.shape[0], D), jnp.float32)
    moe, unused = lax.scan(add_slot, start, (w_gate, w_up, w_down, jnp.arange(SLOTS, dtype=jnp.int32)))
    return (wide + moe).astype(jnp.bfloat16)
```

```python
import functools

import jax
import jax.numpy as jnp
from jax import lax
from jax.experimental import pallas as pl
from jax.experimental.pallas import tpu as pltpu
from jax.sharding import PartitionSpec as P

HEAD_DIM = 128
CAP = 12
LANES = 128
FBLOCK = 256
BF16 = jnp.bfloat16
F32 = jnp.float32
MIB = 2**20
VMEM = pl.BlockSpec(memory_space=pltpu.VMEM)
SMEM = pl.BlockSpec(memory_space=pltpu.SMEM)
ANY = pl.BlockSpec(memory_space=pl.ANY)


def cost(flops, moved):
    return pl.CostEstimate(flops=int(flops), bytes_accessed=int(moved), transcendentals=0)


def place_of(position, count):
    bits = count.bit_length() - 1
    return sum(((position >> b) & 1) << (bits - 1 - b) for b in range(bits))


def swap(value, axis, count, mask):
    return lax.ppermute(value, axis, [(i, i ^ mask) for i in range(count)])


def columns(start, size):
    return pl.ds(pl.multiple_of(start, LANES), size)


def attend_body(
    sides, steps, length, query, new_key, new_value, keys, values, resid, route, *rest
):
    outs, (spread, mixed, key32, value32) = rest[:sides], rest[sides:]
    games, width = query.shape
    heads = width // HEAD_DIM
    wide = new_key.shape[1]
    repeat = heads * HEAD_DIM // wide
    block = keys.shape[0]
    positions = keys.shape[1]
    scale = 1.0 / HEAD_DIM**0.5
    step = pl.program_id(0)

    @pl.when(step == 0)
    def _():
        spread[...] = jnp.zeros_like(spread)
        for h in range(heads):
            lane = h // repeat * HEAD_DIM
            spread[:, h, lane : lane + HEAD_DIM] = query[
                :, h * HEAD_DIM : (h + 1) * HEAD_DIM
            ].astype(F32)
        key32[...] = new_key[...].astype(F32)
        value32[...] = new_value[...].astype(F32)

    for i in range(block):
        game = step * block + i
        q = spread[game]
        score = (
            lax.dot_general(
                q.astype(BF16), keys[i], (((1,), (1,)), ((), ())), preferred_element_type=F32
            )
            * scale
        )
        own = jnp.sum(q * key32[pl.ds(game, 1), :], axis=-1, keepdims=True) * scale
        at = lax.broadcasted_iota(jnp.int32, score.shape, 1)
        score = jnp.where(at < length[game], score, -jnp.inf)
        top = jnp.maximum(jnp.max(score, axis=-1, keepdims=True), own)
        e = jnp.exp(score - top)
        own_e = jnp.exp(own - top)
        total = jnp.sum(e, axis=-1, keepdims=True) + own_e
        prob = (e / total).astype(BF16)
        own_prob = (own_e / total).astype(BF16).astype(F32)
        mixed[game] = (
            jnp.dot(prob, values[i], preferred_element_type=F32)
            + own_prob * value32[pl.ds(game, 1), :]
        )

    @pl.when(step == steps - 1)
    def _():
        side, tensor = lax.axis_index("side"), lax.axis_index("tensor")
        for h in range(heads):
            lane = h // repeat * HEAD_DIM
            part = mixed[:, h, lane : lane + HEAD_DIM].astype(BF16)
            for out in outs:
                out[:, h * HEAD_DIM : (h + 1) * HEAD_DIM] = part
        extra = outs[0].shape[1] - width - LANES
        row = lax.broadcasted_iota(jnp.int32, (games, games), 0)
        diagonal = row == lax.broadcasted_iota(jnp.int32, (games, games), 1)
        lane = lax.broadcasted_iota(jnp.int32, (games, LANES), 1)
        routes = jnp.zeros((games, LANES), F32)
        for j in range(route.shape[0]):
            ids = jnp.broadcast_to(route[j : j + 1, :].astype(F32), (games, games))
            column = jnp.sum(jnp.where(diagonal, ids, 0.0), axis=-1, keepdims=True)
            routes = jnp.where(lane == j, column, routes)
        features = resid.shape[1] // sides
        for k, out in enumerate(outs):
            start = jnp.bitwise_xor(side, k) * features + tensor * extra
            out[:, width : width + extra] = resid[:, columns(start, extra)]
            out[:, width + extra :] = routes.astype(BF16)


def attend(sides, extra, query, new_key, new_value, key_cache, value_cache, cache_len, resid, route_ids):
    games, width = query.shape
    positions, wide = key_cache.shape[1:]
    block = 4
    steps = games // block
    heads = -(-(width // HEAD_DIM) // 16) * 16
    whole = lambda i: (0, 0)
    out = jax.ShapeDtypeStruct((games, width + extra + LANES), BF16)
    return pl.pallas_call(
        functools.partial(attend_body, sides, steps),
        grid=(steps,),
        in_specs=[
            SMEM,
            pl.BlockSpec(query.shape, whole),
            pl.BlockSpec(new_key.shape, whole),
            pl.BlockSpec(new_value.shape, whole),
            pl.BlockSpec((block, positions, wide), lambda i: (i, 0, 0)),
            pl.BlockSpec((block, positions, wide), lambda i: (i, 0, 0)),
            pl.BlockSpec(resid.shape, whole),
            pl.BlockSpec(route_ids.shape[::-1], whole),
        ],
        out_specs=[pl.BlockSpec(out.shape, whole)] * sides,
        out_shape=[out] * sides,
        scratch_shapes=[
            pltpu.VMEM((games, heads, wide), F32),
            pltpu.VMEM((games, heads, wide), F32),
            pltpu.VMEM((games, wide), F32),
            pltpu.VMEM((games, wide), F32),
        ],
        compiler_params=pltpu.CompilerParams(vmem_limit_bytes=10 * MIB),
        cost_estimate=cost(4 * games * heads * positions * wide, 2 * key_cache.size * 2),
        name="attend",
    )(cache_len, query, new_key, new_value, key_cache, value_cache, resid, route_ids.T)


def project_body(sides, tensors, *refs):
    blocks, weight = refs[:sides], refs[sides]
    outs, (rows, total) = refs[sides + 1 : sides + 1 + tensors], refs[sides + 1 + tensors :]
    games = blocks[0].shape[0]
    depth, width = weight.shape
    for p in range(sides):
        rows[p * games : (p + 1) * games, :] = blocks[place_of(p, sides)][:, :depth]
    step = 512 if width % 512 == 0 else LANES
    for c in range(0, width, step):
        total[:, c : c + step] = jnp.dot(
            rows[...], weight[:, c : c + step], preferred_element_type=F32
        )
    tensor = lax.axis_index("tensor")
    part = width // tensors
    for k, out in enumerate(outs):
        start = jnp.bitwise_xor(tensor, k) * part
        out[...] = total[:, columns(start, part)].astype(out.dtype)


def project(sides, tensors, blocks, w_out):
    rows = blocks[0].shape[0] * sides
    depth, width = w_out.shape
    part = width // tensors
    shapes = [jax.ShapeDtypeStruct((rows, part), F32 if k == 0 else BF16) for k in range(tensors)]
    return pl.pallas_call(
        functools.partial(project_body, sides, tensors),
        in_specs=[VMEM] * (sides + 1),
        out_specs=[VMEM] * tensors,
        out_shape=shapes,
        scratch_shapes=[pltpu.VMEM((rows, depth), BF16), pltpu.VMEM((rows, width), F32)],
        compiler_params=pltpu.CompilerParams(vmem_limit_bytes=10 * MIB),
        cost_estimate=cost(2 * rows * depth * width, 2 * depth * width),
        name="project",
    )(*blocks, w_out)


def stream_body(sides, tensors, depth, *refs):
    parts, blocks, out = refs[:tensors], refs[tensors : tensors + sides], refs[-1]
    games = blocks[0].shape[0]
    width = out.shape[1]
    total = parts[0][...]
    for part in parts[1:]:
        total = total + part[...].astype(F32)
    for p in range(sides):
        resid = blocks[place_of(p, sides)][:, depth : depth + width].astype(F32)
        out[p * games : (p + 1) * games, :] = (
            resid + total[p * games : (p + 1) * games, :]
        ).astype(BF16)


def stream_of(sides, tensors, depth, parts, blocks):
    return pl.pallas_call(
        functools.partial(stream_body, sides, tensors, depth),
        in_specs=[VMEM] * (sides + tensors),
        out_specs=VMEM,
        out_shape=jax.ShapeDtypeStruct(parts[0].shape, BF16),
        compiler_params=pltpu.CompilerParams(vmem_limit_bytes=4 * MIB),
        name="stream",
    )(*parts, *blocks)


def gather_body(tensors, *refs):
    out = refs[-1]
    width = refs[0].shape[1]
    tensor = lax.axis_index("tensor")
    for k in range(tensors):
        out[:, columns(jnp.bitwise_xor(tensor, k) * width, width)] = refs[k][...]


def gather_columns(tensors, parts):
    rows, width = parts[0].shape
    return pl.pallas_call(
        functools.partial(gather_body, tensors),
        in_specs=[VMEM] * tensors,
        out_specs=VMEM,
        out_shape=jax.ShapeDtypeStruct((rows, width * tensors), BF16),
        compiler_params=pltpu.CompilerParams(vmem_limit_bytes=4 * MIB),
        name="columns",
    )(*parts)


def prefetch_body(first, count, per_slot, w_gate, w_up, after, out, sems):
    del after
    copies = []
    for i in range(count):
        slot, block = divmod(first + i, per_slot)
        for j, weight in enumerate((w_gate, w_up)):
            copies.append(
                pltpu.make_async_copy(
                    weight.at[slot, :, pl.ds(block * FBLOCK, FBLOCK)],
                    out.at[i, j],
                    sems.at[2 * i + j],
                )
            )
    for c in copies:
        c.start()
    for c in copies:
        c.wait()


def prefetch(first, count, w_gate, w_up, after):
    _, depth, hidden = w_gate.shape
    return pl.pallas_call(
        functools.partial(prefetch_body, first, count, hidden // FBLOCK),
        in_specs=[ANY, ANY, ANY],
        out_specs=VMEM,
        out_shape=pltpu.VMEM((count, 2, depth, FBLOCK), BF16),
        scratch_shapes=[pltpu.SemaphoreType.DMA((2 * count,))],
        compiler_params=pltpu.CompilerParams(vmem_limit_bytes=MIB),
        cost_estimate=cost(0, count * 2 * depth * FBLOCK * 2),
        name="prefetch",
    )(w_gate, w_up, after)


def expand_body(sides, held, depth, split, ring, *refs):
    chunks, refs = refs[:sides], refs[sides:]
    blocks, refs = refs[:sides], refs[sides:]
    gain, router, w_gate, w_up = refs[:4]
    ready, refs = refs[4 : 4 + len(held)], refs[4 + len(held) :]
    inner, mine, stream, rows, router2, scale, buffer, sems = refs
    games = blocks[0].shape[0]
    count = games * sides
    width = chunks[0].shape[1]
    features = width * sides
    slots, _, hidden = w_gate.shape
    per_slot = hidden // FBLOCK
    total_steps = slots * per_slot
    kept = sum(held)
    streamed = total_steps - kept
    side, tensor = lax.axis_index("side"), lax.axis_index("tensor")

    def copies(step, half):
        index = kept + step
        weight = (w_gate, w_up)[half]
        slot = (2 * step + half) % ring
        return pltpu.make_async_copy(
            weight.at[index // per_slot, :, columns(index % per_slot * FBLOCK, FBLOCK)],
            buffer.at[slot],
            sems.at[slot],
        )

    for u in range(min(ring, 2 * streamed)):
        copies(u // 2, u % 2).start()

    power = jnp.zeros((count, LANES), F32)
    for k in range(sides):
        base = jnp.bitwise_xor(side, k) * width
        flip = place_of(k, sides)
        for p in range(sides):
            q = p ^ flip
            stream[p * games : (p + 1) * games, columns(base, width)] = chunks[k][
                q * games : (q + 1) * games, :
            ]
    for c in range(0, features, LANES):
        wide = stream[:, c : c + LANES].astype(F32)
        power = power + wide * wide
    norm = lax.rsqrt(jnp.sum(power, axis=-1, keepdims=True) / features + 1e-05)
    experts = router.shape[0]
    for c in range(0, features, 512):
        s = slice(c, c + 512)
        normed = stream[:, s].astype(F32) * norm * gain[:, s].astype(F32)
        high = normed.astype(BF16)
        rows[:count, s] = high
        rows[count:, s] = (normed - high.astype(F32)).astype(BF16)
        weight = router[:, s]
        top = weight.astype(BF16).astype(F32)
        router2[:, s] = jnp.concatenate([top, weight - top], axis=0).astype(BF16)
    products = lax.dot_general(
        rows[...], router2[...], (((1,), (1,)), ((), ())), preferred_element_type=F32
    )
    products = products[:count] + products[count:]
    logits = products[:, :experts] + products[:, experts:]
    route = jnp.concatenate(
        [blocks[place_of(p, sides)][:, -LANES:] for p in range(sides)], axis=0
    ).astype(F32)
    lane = lax.broadcasted_iota(jnp.int32, route.shape, 1)
    ids = [jnp.sum(jnp.where(lane == j, route, 0.0), axis=-1, keepdims=True) for j in range(2)]
    number = lax.broadcasted_iota(jnp.int32, logits.shape, 1).astype(F32)
    chosen = [
        jnp.sum(jnp.where(number == ids[j], logits, 0.0), axis=-1, keepdims=True)
        for j in range(2)
    ]
    shares = [
        1.0 / (1.0 + jnp.exp(chosen[1] - chosen[0])),
        1.0 / (1.0 + jnp.exp(chosen[0] - chosen[1])),
    ]
    for i in range(slots):
        expert = ((side * slots + i) // split).astype(F32)
        weight = jnp.where(ids[0] == expert, shares[0], 0.0) + jnp.where(
            ids[1] == expert, shares[1], 0.0
        )
        scale[i] = jnp.broadcast_to(weight, (count, FBLOCK))
    mine[...] = stream[:games, columns(tensor * mine.shape[1], mine.shape[1])]

    def finish(index, gate, upward):
        value = gate / (1.0 + jnp.exp(-gate)) * upward * scale[index // per_slot]
        inner[:, columns(index * FBLOCK, FBLOCK)] = value.astype(BF16)

    def product(weight):
        return jnp.dot(rows[:count], weight, preferred_element_type=F32)

    def from_ring(step):
        parts = []
        for half in range(2):
            slot = (2 * step + half) % ring
            copies(step, half).wait()
            parts.append(product(buffer[slot]))

            @pl.when(2 * step + half + ring < 2 * streamed)
            def _():
                copies(step + ring // 2, half).start()

        finish(kept + step, *parts)

    def run(first, last):
        if last > first:
            pl.loop(first, last)(from_ring)

    done = 0
    index = 0
    for array, n in zip(ready, held, strict=True):
        for i in range(n):
            finish(jnp.int32(index), product(array[i, 0]), product(array[i, 1]))
            index += 1
            until = streamed * index // kept
            run(done, until)
            done = until
    run(done, streamed)


def expand(sides, split, chunks, blocks, gain, router, w_gate, w_up, held, ready, own_width):
    games = blocks[0].shape[0]
    count = games * sides
    features = chunks[0].shape[1] * sides
    slots, _, hidden = w_gate.shape
    ring = 4
    moved = 2 * w_gate.size * 2
    return pl.pallas_call(
        functools.partial(expand_body, sides, held, 0, split, ring),
        in_specs=[VMEM] * (2 * sides + 2) + [ANY, ANY] + [VMEM] * len(ready),
        out_specs=[VMEM, VMEM],
        out_shape=[
            jax.ShapeDtypeStruct((count, slots * hidden), BF16),
            jax.ShapeDtypeStruct((games, own_width), BF16),
        ],
        scratch_shapes=[
            pltpu.VMEM((count, features), BF16),
            pltpu.VMEM((2 * count, features), BF16),
            pltpu.VMEM((2 * router.shape[0], features), BF16),
            pltpu.VMEM((slots, count, FBLOCK), F32),
            pltpu.VMEM((ring, features, FBLOCK), BF16),
            pltpu.SemaphoreType.DMA((ring,)),
        ],
        compiler_params=pltpu.CompilerParams(vmem_limit_bytes=20 * MIB),
        cost_estimate=cost(4 * count * w_gate.size, moved),
        name="expand",
    )(*chunks, *blocks, gain, router, w_gate, w_up, *ready)


def contract_body(tensors, ring, block, inner, w_down, keep, send, buffer, sems):
    slots, hidden, features = w_down.shape
    tensor = lax.axis_index("tensor")
    part = features // tensors
    per_part = part // block
    steps = features // block
    half = keep.shape[0]

    def copies(step, slot):
        at = (slots * step + slot) % ring
        k = step // per_part
        start = jnp.bitwise_xor(tensor, k) * part + step % per_part * block
        return pltpu.make_async_copy(
            w_down.at[slot, :, columns(start, block)], buffer.at[at], sems.at[at]
        )

    for u in range(min(ring, slots * steps)):
        copies(u // slots, u % slots).start()

    @pl.loop(0, steps)
    def _(step):
        total = None
        for slot in range(slots):
            copies(step, slot).wait()
            at = (slots * step + slot) % ring
            value = jnp.dot(
                inner[:, slot * hidden : (slot + 1) * hidden],
                buffer[at],
                preferred_element_type=F32,
            )
            total = value if total is None else total + value

            @pl.when(slots * step + slot + ring < slots * steps)
            def _():
                copies(step + ring // slots, slot).start()

        where = columns(step * block, block)
        keep[:, where] = total[:half]
        send[:, where] = total[half:].astype(BF16)


def contract(tensors, inner, w_down):
    count = inner.shape[0]
    slots, hidden, features = w_down.shape
    ring = 6
    block = 512 if features // tensors % 512 == 0 else LANES
    return pl.pallas_call(
        functools.partial(contract_body, tensors, ring, block),
        in_specs=[VMEM, ANY],
        out_specs=[VMEM, VMEM],
        out_shape=[
            jax.ShapeDtypeStruct((count // 2, features), F32),
            jax.ShapeDtypeStruct((count // 2, features), BF16),
        ],
        scratch_shapes=[
            pltpu.VMEM((ring, hidden, block), BF16),
            pltpu.SemaphoreType.DMA((ring,)),
        ],
        compiler_params=pltpu.CompilerParams(vmem_limit_bytes=18 * MIB),
        cost_estimate=cost(2 * count * w_down.size, 2 * w_down.size),
        name="contract",
    )(inner, w_down)


def halve_body(keep, arrived, low, high):
    total = keep[...] + arrived[...].astype(F32)
    half = low.shape[0]
    low[...] = total[:half]
    high[...] = total[half:].astype(BF16)


def halve(keep, arrived):
    rows, width = keep.shape
    return pl.pallas_call(
        halve_body,
        in_specs=[VMEM, VMEM],
        out_specs=[VMEM, VMEM],
        out_shape=[
            jax.ShapeDtypeStruct((rows // 2, width), F32),
            jax.ShapeDtypeStruct((rows // 2, width), BF16),
        ],
        compiler_params=pltpu.CompilerParams(vmem_limit_bytes=6 * MIB),
        name="halve",
    )(keep, arrived)


def deal_body(keep, arrived, *outs):
    width = outs[0].shape[1]
    for k, out in enumerate(outs):
        s = slice(k * width, (k + 1) * width)
        out[...] = (keep[:, s] + arrived[:, s].astype(F32)).astype(out.dtype)


def deal(tensors, keep, arrived):
    rows, width = keep.shape
    return pl.pallas_call(
        deal_body,
        in_specs=[VMEM, VMEM],
        out_specs=[VMEM] * tensors,
        out_shape=[
            jax.ShapeDtypeStruct((rows, width // tensors), F32 if k == 0 else BF16)
            for k in range(tensors)
        ],
        compiler_params=pltpu.CompilerParams(vmem_limit_bytes=4 * MIB),
        name="deal",
    )(keep, arrived)


def last_body(*refs):
    stream, parts, out = refs[0], refs[1:-1], refs[-1]
    total = parts[0][...]
    for part in parts[1:]:
        total = total + part[...].astype(F32)
    out[...] = (stream[...].astype(F32) + total).astype(BF16)


def last(stream, parts):
    return pl.pallas_call(
        last_body,
        in_specs=[VMEM] * (1 + len(parts)),
        out_specs=VMEM,
        out_shape=jax.ShapeDtypeStruct(stream.shape, BF16),
        compiler_params=pltpu.CompilerParams(vmem_limit_bytes=4 * MIB),
        name="last",
    )(stream, *parts)


def shards_kernels(
    query,
    new_key,
    new_value,
    key_cache,
    value_cache,
    cache_len,
    resid,
    w_out,
    rms_gain,
    w_router,
    route_ids,
    w_gate,
    w_up,
    w_down,
):
    sides, tensors = lax.axis_size("side"), lax.axis_size("tensor")
    features = resid.shape[1]
    depth = query.shape[1]
    extra = features // (sides * tensors)
    blocks = attend(
        sides, extra, query, new_key, new_value, key_cache, value_cache, cache_len, resid, route_ids
    )
    blocks = [blocks[0]] + [swap(blocks[k], "side", sides, k) for k in range(1, sides)]
    parts = project(sides, tensors, blocks, w_out)
    parts = [parts[0]] + [swap(parts[k], "tensor", tensors, k) for k in range(1, tensors)]
    stream = stream_of(sides, tensors, depth, parts, blocks)
    pieces = [stream] + [swap(stream, "tensor", tensors, k) for k in range(1, tensors)]
    own = gather_columns(tensors, pieces)
    across = swap(own, "side", sides, 2)
    beside = swap(own, "side", sides, 1)
    chunks = [own, beside, across, swap(across, "side", sides, 1)]
    experts = w_router.shape[1]
    slots = w_gate.shape[0]
    split = slots * sides // experts
    held, ready = [], []
    inner, mine = expand(
        sides,
        split,
        chunks,
        blocks,
        rms_gain.reshape(1, features),
        w_router.T,
        w_gate,
        w_up,
        held,
        ready,
        features // tensors,
    )
    keep, send = contract(tensors, inner, w_down)
    low, high = halve(keep, swap(send, "side", sides, 1))
    dealt = deal(tensors, low, swap(high, "side", sides, 2))
    dealt = [dealt[0]] + [swap(dealt[k], "tensor", tensors, k) for k in range(1, tensors)]
    return last(mine, dealt)


def attend_local(query, new_key, new_value, key_cache, value_cache, cache_len):
    count = query.shape[0]
    positions = key_cache.shape[1]
    kv_local = key_cache.shape[2] // HEAD_DIM
    repeat = query.shape[1] // (kv_local * HEAD_DIM)
    queries = query.reshape(count, kv_local, repeat, HEAD_DIM)
    cached_keys = key_cache.reshape(count, positions, kv_local, HEAD_DIM)
    cached_values = value_cache.reshape(count, positions, kv_local, HEAD_DIM)
    scale = 1.0 / HEAD_DIM**0.5
    scores = (
        jnp.einsum("gkrd,gpkd->gkrp", queries, cached_keys, preferred_element_type=jnp.float32)
        * scale
    )
    own_key = new_key.reshape(count, kv_local, HEAD_DIM)
    own_score = (
        jnp.einsum("gkrd,gkd->gkr", queries, own_key, preferred_element_type=jnp.float32) * scale
    )
    valid = jnp.arange(positions, dtype=jnp.int32)[None, :] < cache_len[:, None]
    scores = jnp.where(valid[:, None, None, :], scores, -jnp.inf)
    highest = jnp.maximum(jnp.max(scores, axis=-1), own_score)
    cached_weight = jnp.exp(scores - highest[..., None])
    own_weight = jnp.exp(own_score - highest)
    total = jnp.sum(cached_weight, axis=-1) + own_weight
    cached_weight = (cached_weight / total[..., None]).astype(jnp.bfloat16)
    own_weight = (own_weight / total).astype(jnp.bfloat16)
    mixed = jnp.einsum(
        "gkrp,gpkd->gkrd", cached_weight, cached_values, preferred_element_type=jnp.float32
    )
    own_value = new_value.reshape(count, kv_local, 1, HEAD_DIM).astype(jnp.float32)
    mixed = mixed + own_weight.astype(jnp.float32)[..., None] * own_value
    return mixed.reshape(count, kv_local * repeat * HEAD_DIM).astype(jnp.bfloat16)


def shards(
    query,
    new_key,
    new_value,
    key_cache,
    value_cache,
    cache_len,
    resid,
    w_out,
    rms_gain,
    w_router,
    route_ids,
    w_gate,
    w_up,
    w_down,
):
    attended = attend_local(query, new_key, new_value, key_cache, value_cache, cache_len)
    column_part = jnp.dot(
        lax.all_gather(attended, "side", axis=0, tiled=True),
        w_out,
        preferred_element_type=jnp.float32,
    )
    partial_out = lax.all_to_all(column_part, "side", split_axis=0, concat_axis=1, tiled=True)
    attn_out = lax.psum(partial_out, "tensor")
    stream = (resid.astype(jnp.float32) + attn_out).astype(jnp.bfloat16)
    wide = stream.astype(jnp.float32)
    power = jnp.mean(wide * wide, axis=-1, keepdims=True)
    normed = wide * lax.rsqrt(power + 1e-05) * rms_gain.astype(jnp.float32)
    logits = jnp.dot(normed, w_router, precision=lax.Precision.HIGHEST)
    experts = w_router.shape[1]
    picked = route_ids[:, :, None] == jnp.arange(experts, dtype=jnp.int32)[None, None, :]
    chosen = jnp.sum(jnp.where(picked, logits[:, None, :], 0.0), axis=-1)
    first = 1.0 / (1.0 + jnp.exp(chosen[:, 1] - chosen[:, 0]))
    second = 1.0 / (1.0 + jnp.exp(chosen[:, 0] - chosen[:, 1]))
    pair = jnp.stack([first, second], axis=1)
    weight = jnp.sum(jnp.where(picked, pair[:, :, None], 0.0), axis=1)
    rows = normed.astype(jnp.bfloat16)
    member = jnp.any(picked, axis=1).astype(jnp.int32)
    order_rank = jnp.cumsum(member, axis=0) - member
    capacity = CAP
    placing = (order_rank.T[:, None, :] == jnp.arange(capacity, dtype=jnp.int32)[None, :, None]) & (
        member.T[:, None, :] == 1
    )
    packed = jnp.einsum(
        "ecg,gd->ecd", placing.astype(jnp.bfloat16), rows, preferred_element_type=jnp.float32
    ).astype(jnp.bfloat16)
    side_count = lax.axis_size("side")
    slot_total = max(side_count, experts)
    split_count = slot_total // experts
    slot_local = slot_total // side_count
    width = rows.shape[1]
    packed = jnp.repeat(packed, split_count, axis=0).reshape(
        side_count, slot_local, capacity, width
    )
    arrived = lax.all_to_all(packed, "side", split_axis=0, concat_axis=0, tiled=True)
    gate = jnp.einsum("sjcd,jdf->sjcf", arrived, w_gate, preferred_element_type=jnp.float32)
    upward = jnp.einsum("sjcd,jdf->sjcf", arrived, w_up, preferred_element_type=jnp.float32)
    inner = (jax.nn.silu(gate) * upward).astype(jnp.bfloat16)
    expert_part = jnp.einsum("sjcf,jfd->sjcd", inner, w_down, preferred_element_type=jnp.float32)
    scaled_place = placing.astype(jnp.float32) * weight.T[:, None, :]
    returned = lax.all_to_all(expert_part, "side", split_axis=0, concat_axis=0, tiled=True)
    features = returned.shape[3]
    merged = jnp.sum(returned.reshape(experts, split_count, capacity, features), axis=1)
    moe = lax.psum_scatter(
        jnp.einsum("ecg,ecf->gf", scaled_place, merged, precision=lax.Precision.HIGHEST),
        "tensor",
        scatter_dimension=1,
        tiled=True,
    )
    columns = moe.shape[1]
    local_stream = lax.dynamic_slice_in_dim(wide, lax.axis_index("tensor") * columns, columns, 1)
    return (local_stream + moe).astype(jnp.bfloat16)


def tiles(mesh, sides=4):
    side, tensor = mesh.shape["side"], mesh.shape["tensor"]
    return side == sides and tensor & (tensor - 1) == 0


def solution(mesh):
    return jax.shard_map(
        shards_kernels if tiles(mesh) else shards,
        mesh=mesh,
        in_specs=(
            P(("groups", "side"), "tensor"),
            P(("groups", "side"), "tensor"),
            P(("groups", "side"), "tensor"),
            P(("groups", "side"), None, "tensor"),
            P(("groups", "side"), None, "tensor"),
            P(("groups", "side")),
            P(("groups", "side"), None),
            P("tensor", "side"),
            P(),
            P(),
            P(("groups", "side"), None),
            P("side", None, "tensor"),
            P("side", None, "tensor"),
            P("side", "tensor", None),
        ),
        out_specs=P(("groups", "side"), "tensor"),
        check_vma=False,
    )
```

```python
import functools
import math

import jax
import jax.numpy as jnp
from jax import lax
from jax.experimental import pallas as pl
from jax.experimental.pallas import tpu as pltpu
from jax.sharding import PartitionSpec as P

HEAD_DIM = 128
CAP = 12
LANES = 128
FBLOCK = 256
BF16 = jnp.bfloat16
F32 = jnp.float32
SCOPE = 8 * 2**20
VMEM = pl.BlockSpec(memory_space=pltpu.VMEM)
SMEM = pl.BlockSpec(memory_space=pltpu.SMEM)
ANY = pl.BlockSpec(memory_space=pl.ANY)
HBM = pl.BlockSpec(memory_space=pltpu.HBM)


def cost(flops, moved):
    return pl.CostEstimate(flops=int(flops), bytes_accessed=int(moved), transcendentals=0)


def place_of(position, count):
    bits = count.bit_length() - 1
    return sum(((position >> b) & 1) << (bits - 1 - b) for b in range(bits))


def swap(value, axis, count, mask):
    return lax.ppermute(value, axis, [(i, i ^ mask) for i in range(count)])


def in_hbm(*arrays):
    return [pltpu.with_memory_space_constraint(a, pltpu.HBM) for a in arrays]


def in_vmem(*arrays):
    return [pltpu.with_memory_space_constraint(a, pltpu.VMEM) for a in arrays]


def columns(start, size):
    return pl.ds(pl.multiple_of(start, LANES), size)


def attend_body(
    sides,
    block,
    length,
    query_at,
    new_key_at,
    new_value_at,
    keys_at,
    values_at,
    resid_at,
    route_at,
    w_out_at,
    *rest,
):
    outs, w_out, rest = rest[:sides], rest[sides], rest[sides + 1 :]
    query, new_key, new_value, keys, values, resid, route, sems, rest = *rest[:8], rest[8:]
    spread, mixed, score, own_score, key32, value32 = rest
    games, width = query.shape
    heads = width // HEAD_DIM
    padded = spread.shape[1]
    wide = new_key.shape[1]
    repeat = heads * HEAD_DIM // wide
    scale = 1.0 / HEAD_DIM**0.5
    steps = games // block

    def copy(source, target, sem):
        return pltpu.make_async_copy(source, target, sems.at[sem])

    small = [
        copy(source, target, i)
        for i, (source, target) in enumerate(
            (
                (query_at, query),
                (new_key_at, new_key),
                (new_value_at, new_value),
                (route_at, route),
                (resid_at, resid),
            )
        )
    ]
    caches = [
        [
            copy(source.at[pl.ds(i * block, block)], target.at[pl.ds(i * block, block)], sem + i)
            for i in range(steps)
        ]
        for source, target, sem in ((keys_at, keys, 5), (values_at, values, 5 + steps))
    ]
    after = copy(w_out_at, w_out, 5 + 2 * steps)
    for c in small[:4] + caches[0] + caches[1] + small[4:] + [after]:
        c.start()
    spread[...] = jnp.zeros_like(spread)
    for c in small[:4]:
        c.wait()
    for h in range(heads):
        lane = h // repeat * HEAD_DIM
        spread[:, h, lane : lane + HEAD_DIM] = query[
            :, h * HEAD_DIM : (h + 1) * HEAD_DIM
        ].astype(F32)
    key32[...] = new_key[...].astype(F32)
    value32[...] = new_value[...].astype(F32)
    for game in range(games):
        if game % block == 0:
            caches[0][game // block].wait()
        q = spread[game]
        s = slice(game * padded, (game + 1) * padded)
        value = (
            lax.dot_general(
                q.astype(BF16), keys[game], (((1,), (1,)), ((), ())), preferred_element_type=F32
            )
            * scale
        )
        at = lax.broadcasted_iota(jnp.int32, value.shape, 1)
        score[s] = jnp.where(at < length[game], value, -jnp.inf)
        own = jnp.sum(q * key32[game : game + 1, :], axis=-1, keepdims=True) * scale
        own_score[s] = jnp.broadcast_to(own, (padded, LANES))
    for i in range(steps):
        s = slice(i * block * padded, (i + 1) * block * padded)
        own = own_score[s][:, :1]
        value = score[s]
        top = jnp.maximum(jnp.max(value, axis=-1, keepdims=True), own)
        e = jnp.exp(value - top)
        own_e = jnp.exp(own - top)
        total = jnp.sum(e, axis=-1, keepdims=True) + own_e
        score[s] = e / total
        own_score[s] = jnp.broadcast_to(
            (own_e / total).astype(BF16).astype(F32), (block * padded, LANES)
        )
        caches[1][i].wait()
        for game in range(i * block, (i + 1) * block):
            s = slice(game * padded, (game + 1) * padded)
            mixed[game] = (
                jnp.dot(score[s].astype(BF16), values[game], preferred_element_type=F32)
                + own_score[s][:, :1] * value32[game : game + 1, :]
            )
    small[4].wait()
    side, tensor = lax.axis_index("side"), lax.axis_index("tensor")
    for h in range(heads):
        lane = h // repeat * HEAD_DIM
        part = mixed[:, h, lane : lane + HEAD_DIM].astype(BF16)
        for out in outs:
            out[:, h * HEAD_DIM : (h + 1) * HEAD_DIM] = part
    extra = outs[0].shape[1] - width - LANES
    row = lax.broadcasted_iota(jnp.int32, (games, games), 0)
    diagonal = row == lax.broadcasted_iota(jnp.int32, (games, games), 1)
    lane = lax.broadcasted_iota(jnp.int32, (games, LANES), 1)
    routes = jnp.zeros((games, LANES), F32)
    for j in range(route.shape[0]):
        ids = jnp.broadcast_to(route[j : j + 1, :].astype(F32), (games, games))
        column = jnp.sum(jnp.where(diagonal, ids, 0.0), axis=-1, keepdims=True)
        routes = jnp.where(lane == j, column, routes)
    features = resid.shape[1] // sides
    for k, out in enumerate(outs):
        start = jnp.bitwise_xor(side, k) * features + tensor % 2 * extra
        out[:, width : width + extra] = resid[:, columns(start, extra)]
        out[:, width + extra :] = routes.astype(BF16)
    after.wait()


def attend(
    sides, extra, query, new_key, new_value, key_cache, value_cache, cache_len, resid, route_ids, w_out
):
    games, width = query.shape
    positions, wide = key_cache.shape[1:]
    block = 4
    heads = -(-(width // HEAD_DIM) // 16) * 16
    out = jax.ShapeDtypeStruct((games, width + extra + LANES), BF16)
    routes = route_ids.T
    arrays = [query, new_key, new_value, key_cache, value_cache, resid, routes]
    return pl.pallas_call(
        functools.partial(attend_body, sides, block),
        in_specs=[SMEM] + [HBM] * (len(arrays) + 1),
        out_specs=[VMEM] * (sides + 1),
        out_shape=[out] * sides + [pltpu.VMEM(w_out.shape, BF16)],
        scratch_shapes=[pltpu.VMEM(a.shape, a.dtype) for a in arrays]
        + [
            pltpu.SemaphoreType.DMA((6 + 2 * (games // block),)),
            pltpu.VMEM((games, heads, wide), F32),
            pltpu.VMEM((games, heads, wide), F32),
            pltpu.VMEM((games * heads, positions), F32),
            pltpu.VMEM((games * heads, LANES), F32),
            pltpu.VMEM((games, wide), F32),
            pltpu.VMEM((games, wide), F32),
        ],
        compiler_params=pltpu.CompilerParams(vmem_limit_bytes=SCOPE),
        cost_estimate=cost(4 * games * heads * positions * wide, 2 * key_cache.size * 2),
        name="attend",
    )(cache_len, *in_hbm(*arrays, w_out))


def project_body(sides, *refs):
    blocks, weight = refs[:sides], refs[sides]
    mine, other, rows, total = refs[sides + 2 :]
    games = blocks[0].shape[0]
    depth, width = weight.shape
    for p in range(sides):
        rows[p * games : (p + 1) * games, :] = blocks[place_of(p, sides)][:, :depth]
    step = 512 if width % 512 == 0 else LANES
    for c in range(0, width, step):
        total[:, c : c + step] = jnp.dot(
            rows[...], weight[:, c : c + step], preferred_element_type=F32
        )
    odd = lax.axis_index("tensor") % 2
    half = width // 2
    mine[...] = total[:, columns(odd * half, half)]
    other[...] = total[:, columns((1 - odd) * half, half)].astype(BF16)


def project(sides, blocks, w_out, after):
    rows = blocks[0].shape[0] * sides
    depth, width = w_out.shape
    return pl.pallas_call(
        functools.partial(project_body, sides),
        in_specs=[VMEM] * (sides + 2),
        out_specs=[VMEM] * 2,
        out_shape=[
            jax.ShapeDtypeStruct((rows, width // 2), F32),
            jax.ShapeDtypeStruct((rows, width // 2), BF16),
        ],
        scratch_shapes=[pltpu.VMEM((rows, depth), BF16), pltpu.VMEM((rows, width), F32)],
        compiler_params=pltpu.CompilerParams(vmem_limit_bytes=SCOPE),
        cost_estimate=cost(2 * rows * depth * width, 2 * depth * width),
        name="project",
    )(*blocks, *in_vmem(w_out, after))


def add_body(mine, arrived, after, total, rounded):
    del after
    value = mine[...] + arrived[...].astype(F32)
    total[...] = value
    rounded[...] = value.astype(BF16)


def add(mine, arrived, after):
    return pl.pallas_call(
        add_body,
        in_specs=[VMEM, VMEM, VMEM],
        out_specs=[VMEM] * 2,
        out_shape=[
            jax.ShapeDtypeStruct(mine.shape, F32),
            jax.ShapeDtypeStruct(mine.shape, BF16),
        ],
        compiler_params=pltpu.CompilerParams(vmem_limit_bytes=SCOPE),
        name="add",
    )(mine, arrived, *in_vmem(after))


def stream_body(sides, depth, mine, arrived, *refs):
    blocks, out = refs[:sides], refs[-1]
    games = blocks[0].shape[0]
    width = out.shape[1]
    for p in range(sides):
        s = slice(p * games, (p + 1) * games)
        resid = blocks[place_of(p, sides)][:, depth : depth + width].astype(F32)
        out[s, :] = (resid + (mine[s] + arrived[s].astype(F32))).astype(BF16)


def stream_of(sides, depth, mine, arrived, blocks, after):
    return pl.pallas_call(
        functools.partial(stream_body, sides, depth),
        in_specs=[VMEM] * (sides + 3),
        out_specs=VMEM,
        out_shape=jax.ShapeDtypeStruct(mine.shape, BF16),
        compiler_params=pltpu.CompilerParams(vmem_limit_bytes=SCOPE),
        name="stream",
    )(mine, arrived, *blocks, *in_vmem(after))


def join_body(mine, arrived, out):
    width = mine.shape[1]
    odd = lax.axis_index("tensor") % 2
    out[:, columns(odd * width, width)] = mine[...]
    out[:, columns((1 - odd) * width, width)] = arrived[...]


def join(mine, arrived):
    rows, width = mine.shape
    return pl.pallas_call(
        join_body,
        in_specs=[VMEM] * 2,
        out_specs=VMEM,
        out_shape=jax.ShapeDtypeStruct((rows, 2 * width), BF16),
        compiler_params=pltpu.CompilerParams(vmem_limit_bytes=SCOPE),
        name="join",
    )(mine, arrived)


def prefetch_body(first, per_slot, w_gate, w_up, after, out, sems):
    del after
    copies = []
    for i in range(out.shape[0]):
        slot, block = divmod(first + i, per_slot)
        for half, weight in enumerate((w_gate, w_up)):
            copies.append(
                pltpu.make_async_copy(
                    weight.at[slot, :, pl.ds(block * FBLOCK, FBLOCK)],
                    out.at[i, half],
                    sems.at[i, half],
                )
            )
    for c in copies:
        c.start()
    for c in copies:
        c.wait()


def prefetch(first, count, w_gate, w_up, after):
    _, depth, hidden = w_gate.shape
    return pl.pallas_call(
        functools.partial(prefetch_body, first, hidden // FBLOCK),
        in_specs=[HBM, HBM, VMEM],
        out_specs=VMEM,
        out_shape=pltpu.VMEM((count, 2, depth, FBLOCK), BF16),
        scratch_shapes=[pltpu.SemaphoreType.DMA((count, 2))],
        compiler_params=pltpu.CompilerParams(vmem_limit_bytes=SCOPE),
        cost_estimate=cost(0, count * 2 * depth * FBLOCK * 2),
        name="prefetch",
    )(*in_hbm(w_gate, w_up), after)


def halves(value, gain, rows, where):
    count = value.shape[0]
    scaled = value.astype(F32) * gain.astype(F32)
    high = scaled.astype(BF16)
    rows[:count, where] = high
    rows[count:, where] = (scaled - high.astype(F32)).astype(BF16)


def fold(value):
    count = value.shape[0] // 2
    return value[:count] + value[count:]


def expand_body(sides, held, split, ring, *refs):
    chunks, refs = refs[:sides], refs[sides:]
    blocks, refs = refs[:sides], refs[sides:]
    gain, router, w_gate, w_up = refs[:4]
    ready, refs = refs[4 : 4 + len(held)], refs[4 + len(held) :]
    inner, mine, stream, rows, router2, scale, norms, raw, buffer, sems = refs
    games = blocks[0].shape[0]
    count = games * sides
    width = chunks[0].shape[1]
    features = width * sides
    slots, _, hidden = w_gate.shape
    per_slot = hidden // FBLOCK
    kept = sum(held)
    streamed = slots * per_slot - kept
    side, tensor = lax.axis_index("side"), lax.axis_index("tensor")

    def copies(step):
        index = kept + step
        return [
            pltpu.make_async_copy(
                weight.at[index // per_slot, :, columns(index % per_slot * FBLOCK, FBLOCK)],
                buffer.at[step % ring, half],
                sems.at[step % ring, half],
            )
            for half, weight in enumerate((w_gate, w_up))
        ]

    for step in range(min(ring, streamed)):
        for c in copies(step):
            c.start()

    power = jnp.zeros((count, LANES), F32)
    experts = router.shape[0]
    for k in range(sides):
        base = jnp.bitwise_xor(side, k) * width
        flip = place_of(k, sides)
        for c in range(0, width, 512):
            value = jnp.concatenate(
                [
                    chunks[k][(p ^ flip) * games : (p ^ flip) * games + games, c : c + 512]
                    for p in range(sides)
                ],
                axis=0,
            )
            wide = value.astype(F32)
            for i in range(0, 512, LANES):
                power = power + wide[:, i : i + LANES] * wide[:, i : i + LANES]
            there = columns(base + c, 512)
            stream[:, there] = value[:games]
            halves(value, gain[:, there], rows, there)
            weight = router[:, there]
            top = weight.astype(BF16).astype(F32)
            router2[:, there] = jnp.concatenate([top, weight - top], axis=0).astype(BF16)
    norm = lax.rsqrt(jnp.sum(power, axis=-1, keepdims=True) / features + 1e-05)
    norms[...] = jnp.broadcast_to(norm, norms.shape)
    products = fold(
        lax.dot_general(
            rows[...], router2[...], (((1,), (1,)), ((), ())), preferred_element_type=F32
        )
    )
    logits = (products[:, :experts] + products[:, experts:]) * norm
    route = jnp.concatenate(
        [blocks[place_of(p, sides)][:, -LANES:] for p in range(sides)], axis=0
    ).astype(F32)
    lane = lax.broadcasted_iota(jnp.int32, route.shape, 1)
    ids = [jnp.sum(jnp.where(lane == j, route, 0.0), axis=-1, keepdims=True) for j in range(2)]
    number = lax.broadcasted_iota(jnp.int32, logits.shape, 1).astype(F32)
    chosen = [
        jnp.sum(jnp.where(number == ids[j], logits, 0.0), axis=-1, keepdims=True)
        for j in range(2)
    ]
    shares = [
        1.0 / (1.0 + jnp.exp(chosen[1] - chosen[0])),
        1.0 / (1.0 + jnp.exp(chosen[0] - chosen[1])),
    ]
    for i in range(slots):
        expert = ((side * slots + i) // split).astype(F32)
        weight = jnp.where(ids[0] == expert, shares[0], 0.0) + jnp.where(
            ids[1] == expert, shares[1], 0.0
        )
        scale[i] = jnp.broadcast_to(weight, (count, FBLOCK))
    mine[...] = stream[:, columns(tensor * mine.shape[1], mine.shape[1])]

    def products(weights, turn):
        for half in range(2):
            raw[turn % 2, half] = fold(
                jnp.dot(rows[...], weights[half], preferred_element_type=F32)
            )

    def finish(index, turn):
        gate = raw[turn % 2, 0] * norms[...]
        upward = raw[turn % 2, 1] * norms[...]
        value = gate / (1.0 + jnp.exp(-gate)) * upward * scale[index // per_slot]
        where = columns(index * FBLOCK, FBLOCK)
        high = value.astype(BF16)
        inner[:count, where] = high
        inner[count:, where] = (value - high.astype(F32)).astype(BF16)

    def from_ring(step, turn, before):
        for c in copies(step):
            c.wait()
        products(buffer.at[step % ring], turn)
        if before is not None:
            finish(before, turn + 1)

        @pl.when(step + ring < streamed)
        def _():
            for c in copies(step + ring):
                c.start()

    resident = [(array, i) for array, n in zip(ready, held, strict=True) for i in range(n)]
    done, before = 0, None
    for index in range(kept + 1):
        until = streamed * (index + 1) // (kept + 1)
        if done < until:
            from_ring(jnp.int32(done), done + index, before)

            @pl.loop(done + 1, until)
            def _(step):
                from_ring(step, step + index, kept + step - 1)

            done, before = until, kept + until - 1
        if index < kept:
            array, i = resident[index]
            products(array.at[i], done + index)
            if before is not None:
                finish(before, done + index + 1)
            before = index
    finish(before, streamed + kept - 1)


def expand(sides, split, chunks, blocks, gain, router, w_gate, w_up, held, ready, own_width):
    games = blocks[0].shape[0]
    count = games * sides
    features = chunks[0].shape[1] * sides
    slots, _, hidden = w_gate.shape
    ring = 2
    arguments = [*chunks, *blocks, gain, router]
    return pl.pallas_call(
        functools.partial(expand_body, sides, held, split, ring),
        in_specs=[VMEM] * len(arguments) + [HBM] * 2 + [VMEM] * len(ready),
        out_specs=[VMEM] * 2,
        out_shape=[
            jax.ShapeDtypeStruct((2 * count, slots * hidden), BF16),
            jax.ShapeDtypeStruct((games, own_width), BF16),
        ],
        scratch_shapes=[
            pltpu.VMEM((games, features), BF16),
            pltpu.VMEM((2 * count, features), BF16),
            pltpu.VMEM((2 * router.shape[0], features), BF16),
            pltpu.VMEM((slots, count, FBLOCK), F32),
            pltpu.VMEM((count, FBLOCK), F32),
            pltpu.VMEM((2, 2, count, FBLOCK), F32),
            pltpu.VMEM((ring, 2, features, FBLOCK), BF16),
            pltpu.SemaphoreType.DMA((ring, 2)),
        ],
        compiler_params=pltpu.CompilerParams(vmem_limit_bytes=18 * 2**20),
        cost_estimate=cost(8 * count * w_gate.size, 2 * w_gate.size * 2),
        name="expand",
    )(*arguments, *in_hbm(w_gate, w_up), *in_vmem(*ready))


def contract_body(tensors, ring, block, inner, w_down, keep, send, buffer, sems):
    slots, hidden, features = w_down.shape
    tensor = lax.axis_index("tensor")
    part = features // tensors
    per_part = part // block
    steps = features // block
    half = keep.shape[0]
    deep = ring // slots

    def copies(step):
        start = jnp.bitwise_xor(tensor, step // per_part) * part + step % per_part * block
        return [
            pltpu.make_async_copy(
                w_down.at[slot, :, columns(start, block)],
                buffer.at[step % deep, slot],
                sems.at[step % deep, slot],
            )
            for slot in range(slots)
        ]

    for step in range(min(deep, steps)):
        for c in copies(step):
            c.start()

    def run(step, more):
        for c in copies(step):
            c.wait()
        total = None
        for slot in range(slots):
            value = jnp.dot(
                inner[:, slot * hidden : (slot + 1) * hidden],
                buffer[step % deep, slot],
                preferred_element_type=F32,
            )
            total = value if total is None else total + value
        total = fold(total)
        where = columns(step * block, block)
        keep[:, where] = total[:half]
        send[:, where] = total[half:].astype(BF16)
        if more:
            for c in copies(step + deep):
                c.start()

    edge = max(0, steps - deep)
    pl.loop(0, edge)(lambda step: run(step, True))
    for step in range(edge, steps):
        run(step, False)


def contract(tensors, inner, w_down):
    count = inner.shape[0] // 2
    slots, hidden, features = w_down.shape
    ring = 4 * slots
    block = 512 if features // tensors % 512 == 0 else LANES
    return pl.pallas_call(
        functools.partial(contract_body, tensors, ring, block),
        in_specs=[VMEM, HBM],
        out_specs=[VMEM, VMEM],
        out_shape=[
            jax.ShapeDtypeStruct((count // 2, features), F32),
            jax.ShapeDtypeStruct((count // 2, features), BF16),
        ],
        scratch_shapes=[
            pltpu.VMEM((ring // slots, slots, hidden, block), BF16),
            pltpu.SemaphoreType.DMA((ring // slots, slots)),
        ],
        compiler_params=pltpu.CompilerParams(vmem_limit_bytes=24 * 2**20),
        cost_estimate=cost(4 * count * w_down.size, 2 * w_down.size),
        name="contract",
    )(inner, *in_hbm(w_down))


def halve_body(keep, arrived, low, high):
    total = keep[...] + arrived[...].astype(F32)
    half = low.shape[0]
    low[...] = total[:half]
    high[...] = total[half:].astype(BF16)


def halve(keep, arrived):
    rows, width = keep.shape
    return pl.pallas_call(
        halve_body,
        in_specs=[VMEM, VMEM],
        out_specs=[VMEM, VMEM],
        out_shape=[
            jax.ShapeDtypeStruct((rows // 2, width), F32),
            jax.ShapeDtypeStruct((rows // 2, width), BF16),
        ],
        compiler_params=pltpu.CompilerParams(vmem_limit_bytes=SCOPE),
        name="halve",
    )(keep, arrived)


def deal_body(keep, arrived, *outs):
    width = outs[0].shape[1]
    for k, out in enumerate(outs):
        s = slice(k * width, (k + 1) * width)
        out[...] = (keep[:, s] + arrived[:, s].astype(F32)).astype(out.dtype)


def deal(tensors, keep, arrived):
    rows, width = keep.shape
    return pl.pallas_call(
        deal_body,
        in_specs=[VMEM, VMEM],
        out_specs=[VMEM] * tensors,
        out_shape=[
            jax.ShapeDtypeStruct((rows, width // tensors), F32 if k == 0 else BF16)
            for k in range(tensors)
        ],
        compiler_params=pltpu.CompilerParams(vmem_limit_bytes=SCOPE),
        name="deal",
    )(keep, arrived)


def last_body(*refs):
    stream, parts, out = refs[0], refs[1:-1], refs[-1]
    total = parts[0][...]
    for part in parts[1:]:
        total = total + part[...].astype(F32)
    out[...] = (stream[...].astype(F32) + total).astype(BF16)


def last(stream, parts):
    return pl.pallas_call(
        last_body,
        in_specs=[VMEM] * (1 + len(parts)),
        out_specs=VMEM,
        out_shape=jax.ShapeDtypeStruct(stream.shape, BF16),
        compiler_params=pltpu.CompilerParams(vmem_limit_bytes=SCOPE),
        name="last",
    )(stream, *parts)


def shards_kernels(
    query,
    new_key,
    new_value,
    key_cache,
    value_cache,
    cache_len,
    resid,
    w_out,
    rms_gain,
    w_router,
    route_ids,
    w_gate,
    w_up,
    w_down,
):
    sides, tensors = lax.axis_size("side"), lax.axis_size("tensor")
    features = resid.shape[1]
    depth = query.shape[1]
    extra = features // sides // 2
    slots, _, hidden = w_gate.shape
    held = [2, 1, 2]
    *blocks, w_here = attend(
        sides,
        extra,
        query,
        new_key,
        new_value,
        key_cache,
        value_cache,
        cache_len,
        resid,
        route_ids,
        w_out,
    )
    ready = [prefetch(0, held[0], w_gate, w_up, blocks[0])]
    blocks = [blocks[0]] + [swap(blocks[k], "side", sides, k) for k in range(1, sides)]
    mine, other = project(sides, blocks, w_here, ready[0])
    ready.append(prefetch(held[0], held[1], w_gate, w_up, other))
    mine, other = add(mine, swap(other, "tensor", tensors, 1), ready[1])
    ready.append(prefetch(held[0] + held[1], held[2], w_gate, w_up, other))
    step = 2
    while step < tensors // 2:
        mine, other = add(mine, swap(other, "tensor", tensors, step), ready[2])
        step *= 2
    stream = stream_of(sides, depth, mine, swap(other, "tensor", tensors, step), blocks, ready[2])
    own = join(stream, swap(stream, "tensor", tensors, 1))
    across = swap(own, "side", sides, 2)
    beside = swap(own, "side", sides, 1)
    chunks = [own, beside, across, swap(across, "side", sides, 1)]
    inner, mine = expand(
        sides,
        slots * sides // w_router.shape[1],
        chunks,
        blocks,
        rms_gain.reshape(1, features),
        w_router.T,
        w_gate,
        w_up,
        held,
        ready,
        features // tensors,
    )
    keep, send = contract(tensors, inner, w_down)
    low, high = halve(keep, swap(send, "side", sides, 1))
    dealt = deal(tensors, low, swap(high, "side", sides, 2))
    dealt = [dealt[0]] + [swap(dealt[k], "tensor", tensors, k) for k in range(1, tensors)]
    return last(mine, dealt)


def attend_local(query, new_key, new_value, key_cache, value_cache, cache_len):
    count = query.shape[0]
    positions = key_cache.shape[1]
    kv_local = key_cache.shape[2] // HEAD_DIM
    repeat = query.shape[1] // (kv_local * HEAD_DIM)
    queries = query.reshape(count, kv_local, repeat, HEAD_DIM)
    cached_keys = key_cache.reshape(count, positions, kv_local, HEAD_DIM)
    cached_values = value_cache.reshape(count, positions, kv_local, HEAD_DIM)
    scale = 1.0 / HEAD_DIM**0.5
    scores = (
        jnp.einsum("gkrd,gpkd->gkrp", queries, cached_keys, preferred_element_type=jnp.float32)
        * scale
    )
    own_key = new_key.reshape(count, kv_local, HEAD_DIM)
    own_score = (
        jnp.einsum("gkrd,gkd->gkr", queries, own_key, preferred_element_type=jnp.float32) * scale
    )
    valid = jnp.arange(positions, dtype=jnp.int32)[None, :] < cache_len[:, None]
    scores = jnp.where(valid[:, None, None, :], scores, -jnp.inf)
    highest = jnp.maximum(jnp.max(scores, axis=-1), own_score)
    cached_weight = jnp.exp(scores - highest[..., None])
    own_weight = jnp.exp(own_score - highest)
    total = jnp.sum(cached_weight, axis=-1) + own_weight
    cached_weight = (cached_weight / total[..., None]).astype(jnp.bfloat16)
    own_weight = (own_weight / total).astype(jnp.bfloat16)
    mixed = jnp.einsum(
        "gkrp,gpkd->gkrd", cached_weight, cached_values, preferred_element_type=jnp.float32
    )
    own_value = new_value.reshape(count, kv_local, 1, HEAD_DIM).astype(jnp.float32)
    mixed = mixed + own_weight.astype(jnp.float32)[..., None] * own_value
    return mixed.reshape(count, kv_local * repeat * HEAD_DIM).astype(jnp.bfloat16)


def shards(
    query,
    new_key,
    new_value,
    key_cache,
    value_cache,
    cache_len,
    resid,
    w_out,
    rms_gain,
    w_router,
    route_ids,
    w_gate,
    w_up,
    w_down,
):
    attended = attend_local(query, new_key, new_value, key_cache, value_cache, cache_len)
    column_part = jnp.dot(
        lax.all_gather(attended, "side", axis=0, tiled=True),
        w_out,
        preferred_element_type=jnp.float32,
    )
    partial_out = lax.all_to_all(column_part, "side", split_axis=0, concat_axis=1, tiled=True)
    attn_out = lax.psum(partial_out, "tensor")
    stream = (resid.astype(jnp.float32) + attn_out).astype(jnp.bfloat16)
    wide = stream.astype(jnp.float32)
    power = jnp.mean(wide * wide, axis=-1, keepdims=True)
    normed = wide * lax.rsqrt(power + 1e-05) * rms_gain.astype(jnp.float32)
    logits = jnp.dot(normed, w_router, precision=lax.Precision.HIGHEST)
    experts = w_router.shape[1]
    picked = route_ids[:, :, None] == jnp.arange(experts, dtype=jnp.int32)[None, None, :]
    chosen = jnp.sum(jnp.where(picked, logits[:, None, :], 0.0), axis=-1)
    first = 1.0 / (1.0 + jnp.exp(chosen[:, 1] - chosen[:, 0]))
    second = 1.0 / (1.0 + jnp.exp(chosen[:, 0] - chosen[:, 1]))
    pair = jnp.stack([first, second], axis=1)
    weight = jnp.sum(jnp.where(picked, pair[:, :, None], 0.0), axis=1)
    rows = normed.astype(jnp.bfloat16)
    member = jnp.any(picked, axis=1).astype(jnp.int32)
    order_rank = jnp.cumsum(member, axis=0) - member
    capacity = CAP
    placing = (order_rank.T[:, None, :] == jnp.arange(capacity, dtype=jnp.int32)[None, :, None]) & (
        member.T[:, None, :] == 1
    )
    packed = jnp.einsum(
        "ecg,gd->ecd", placing.astype(jnp.bfloat16), rows, preferred_element_type=jnp.float32
    ).astype(jnp.bfloat16)
    side_count = lax.axis_size("side")
    slot_total = max(side_count, experts)
    split_count = slot_total // experts
    slot_local = slot_total // side_count
    width = rows.shape[1]
    packed = jnp.repeat(packed, split_count, axis=0).reshape(
        side_count, slot_local, capacity, width
    )
    arrived = lax.all_to_all(packed, "side", split_axis=0, concat_axis=0, tiled=True)
    gate = jnp.einsum("sjcd,jdf->sjcf", arrived, w_gate, preferred_element_type=jnp.float32)
    upward = jnp.einsum("sjcd,jdf->sjcf", arrived, w_up, preferred_element_type=jnp.float32)
    inner = (jax.nn.silu(gate) * upward).astype(jnp.bfloat16)
    expert_part = jnp.einsum("sjcf,jfd->sjcd", inner, w_down, preferred_element_type=jnp.float32)
    scaled_place = placing.astype(jnp.float32) * weight.T[:, None, :]
    returned = lax.all_to_all(expert_part, "side", split_axis=0, concat_axis=0, tiled=True)
    features = returned.shape[3]
    merged = jnp.sum(returned.reshape(experts, split_count, capacity, features), axis=1)
    moe = lax.psum_scatter(
        jnp.einsum("ecg,ecf->gf", scaled_place, merged, precision=lax.Precision.HIGHEST),
        "tensor",
        scatter_dimension=1,
        tiled=True,
    )
    columns = moe.shape[1]
    local_stream = lax.dynamic_slice_in_dim(wide, lax.axis_index("tensor") * columns, columns, 1)
    return (local_stream + moe).astype(jnp.bfloat16)


def tiles(mesh, sides=4):
    side, tensor = mesh.shape["side"], mesh.shape["tensor"]
    return side == sides and tensor >= 4 and tensor & (tensor - 1) == 0


def solution(mesh):
    return jax.shard_map(
        shards_kernels if tiles(mesh) else shards,
        mesh=mesh,
        in_specs=(
            P(("groups", "side"), "tensor"),
            P(("groups", "side"), "tensor"),
            P(("groups", "side"), "tensor"),
            P(("groups", "side"), None, "tensor"),
            P(("groups", "side"), None, "tensor"),
            P(("groups", "side")),
            P(("groups", "side"), None),
            P("tensor", "side"),
            P(),
            P(),
            P(("groups", "side"), None),
            P("side", None, "tensor"),
            P("side", None, "tensor"),
            P("side", "tensor", None),
        ),
        out_specs=P(("groups", "side"), "tensor"),
        check_vma=False,
    )
```

```python
import functools
import math

import jax
import jax.numpy as jnp
from jax import lax
from jax.experimental import pallas as pl
from jax.experimental.pallas import tpu as pltpu
from jax.sharding import PartitionSpec as P

HEAD_DIM = 128
CAP = 12
LANES = 128
FBLOCK = 256
BF16 = jnp.bfloat16
F32 = jnp.float32
SCOPE = 8 * 2**20
VMEM = pl.BlockSpec(memory_space=pltpu.VMEM)
ANY = pl.BlockSpec(memory_space=pl.ANY)
HBM = pl.BlockSpec(memory_space=pltpu.HBM)


def cost(flops, moved):
    return pl.CostEstimate(flops=int(flops), bytes_accessed=int(moved), transcendentals=0)


def place_of(position, count):
    bits = count.bit_length() - 1
    return sum(((position >> b) & 1) << (bits - 1 - b) for b in range(bits))


def swap(value, axis, count, mask):
    return lax.ppermute(value, axis, [(i, i ^ mask) for i in range(count)])


def in_hbm(*arrays):
    return [pltpu.with_memory_space_constraint(a, pltpu.HBM) for a in arrays]


def in_vmem(*arrays):
    return [pltpu.with_memory_space_constraint(a, pltpu.VMEM) for a in arrays]


def columns(start, size):
    return pl.ds(pl.multiple_of(start, LANES), size)


def attend_body(
    sides,
    block,
    length_at,
    query_at,
    new_key_at,
    new_value_at,
    keys_at,
    values_at,
    resid_at,
    route_at,
    w_out_at,
    *rest,
):
    outs, w_out, rest = rest[:sides], rest[sides], rest[sides + 1 :]
    query, new_key, new_value, keys, values, resid, route, sems, rest = *rest[:8], rest[8:]
    length, spread, mixed, score, own_score, key32, value32 = rest
    games, width = query.shape
    heads = width // HEAD_DIM
    padded = spread.shape[1]
    wide = new_key.shape[1]
    repeat = heads * HEAD_DIM // wide
    scale = 1.0 / HEAD_DIM**0.5
    steps = games // block

    def copy(source, target, sem):
        return pltpu.make_async_copy(source, target, sems.at[sem])

    small = [
        copy(source, target, i)
        for i, (source, target) in enumerate(
            (
                (query_at, query),
                (new_key_at, new_key),
                (new_value_at, new_value),
                (route_at, route),
                (resid_at, resid),
            )
        )
    ]
    caches = [
        [
            copy(source.at[pl.ds(i * block, block)], target.at[pl.ds(i * block, block)], sem + i)
            for i in range(steps)
        ]
        for source, target, sem in ((keys_at, keys, 5), (values_at, values, 5 + steps))
    ]
    after = copy(w_out_at, w_out, 5 + 2 * steps)
    lengths = copy(length_at, length, 6 + 2 * steps)
    for c in [lengths] + small[:4] + caches[0] + caches[1] + small[4:] + [after]:
        c.start()
    spread[...] = jnp.zeros_like(spread)
    for c in [lengths] + small[:4]:
        c.wait()
    for h in range(heads):
        lane = h // repeat * HEAD_DIM
        spread[:, h, lane : lane + HEAD_DIM] = query[
            :, h * HEAD_DIM : (h + 1) * HEAD_DIM
        ].astype(F32)
    key32[...] = new_key[...].astype(F32)
    value32[...] = new_value[...].astype(F32)
    for game in range(games):
        if game % block == 0:
            caches[0][game // block].wait()
        q = spread[game]
        s = slice(game * padded, (game + 1) * padded)
        value = (
            lax.dot_general(
                q.astype(BF16), keys[game], (((1,), (1,)), ((), ())), preferred_element_type=F32
            )
            * scale
        )
        at = lax.broadcasted_iota(jnp.int32, value.shape, 1)
        score[s] = jnp.where(at < length[game], value, -jnp.inf)
        own = jnp.sum(q * key32[game : game + 1, :], axis=-1, keepdims=True) * scale
        own_score[s] = jnp.broadcast_to(own, (padded, LANES))
    for i in range(steps):
        s = slice(i * block * padded, (i + 1) * block * padded)
        own = own_score[s][:, :1]
        value = score[s]
        top = jnp.maximum(jnp.max(value, axis=-1, keepdims=True), own)
        e = jnp.exp(value - top)
        own_e = jnp.exp(own - top)
        total = jnp.sum(e, axis=-1, keepdims=True) + own_e
        score[s] = e / total
        own_score[s] = jnp.broadcast_to(
            (own_e / total).astype(BF16).astype(F32), (block * padded, LANES)
        )
        caches[1][i].wait()
        for game in range(i * block, (i + 1) * block):
            s = slice(game * padded, (game + 1) * padded)
            mixed[game] = (
                jnp.dot(score[s].astype(BF16), values[game], preferred_element_type=F32)
                + own_score[s][:, :1] * value32[game : game + 1, :]
            )
    small[4].wait()
    side, tensor = lax.axis_index("side"), lax.axis_index("tensor")
    for h in range(heads):
        lane = h // repeat * HEAD_DIM
        part = mixed[:, h, lane : lane + HEAD_DIM].astype(BF16)
        for out in outs:
            out[:, h * HEAD_DIM : (h + 1) * HEAD_DIM] = part
    extra = outs[0].shape[1] - width - LANES
    row = lax.broadcasted_iota(jnp.int32, (games, games), 0)
    diagonal = row == lax.broadcasted_iota(jnp.int32, (games, games), 1)
    lane = lax.broadcasted_iota(jnp.int32, (games, LANES), 1)
    routes = jnp.zeros((games, LANES), F32)
    for j in range(route.shape[0]):
        ids = jnp.broadcast_to(route[j : j + 1, :].astype(F32), (games, games))
        column = jnp.sum(jnp.where(diagonal, ids, 0.0), axis=-1, keepdims=True)
        routes = jnp.where(lane == j, column, routes)
    features = resid.shape[1] // sides
    for k, out in enumerate(outs):
        start = jnp.bitwise_xor(side, k) * features + tensor % 2 * extra
        out[:, width : width + extra] = resid[:, columns(start, extra)]
        out[:, width + extra :] = routes.astype(BF16)
    after.wait()


def attend(
    sides, extra, query, new_key, new_value, key_cache, value_cache, cache_len, resid, route_ids, w_out
):
    games, width = query.shape
    positions, wide = key_cache.shape[1:]
    block = 4
    heads = -(-(width // HEAD_DIM) // 16) * 16
    out = jax.ShapeDtypeStruct((games, width + extra + LANES), BF16)
    routes = route_ids.T
    arrays = [query, new_key, new_value, key_cache, value_cache, resid, routes]
    return pl.pallas_call(
        functools.partial(attend_body, sides, block),
        in_specs=[HBM] * (len(arrays) + 2),
        out_specs=[VMEM] * (sides + 1),
        out_shape=[out] * sides + [pltpu.VMEM(w_out.shape, BF16)],
        scratch_shapes=[pltpu.VMEM(a.shape, a.dtype) for a in arrays]
        + [
            pltpu.SemaphoreType.DMA((7 + 2 * (games // block),)),
            pltpu.SMEM(cache_len.shape, jnp.int32),
            pltpu.VMEM((games, heads, wide), F32),
            pltpu.VMEM((games, heads, wide), F32),
            pltpu.VMEM((games * heads, positions), F32),
            pltpu.VMEM((games * heads, LANES), F32),
            pltpu.VMEM((games, wide), F32),
            pltpu.VMEM((games, wide), F32),
        ],
        compiler_params=pltpu.CompilerParams(vmem_limit_bytes=SCOPE),
        cost_estimate=cost(4 * games * heads * positions * wide, 2 * key_cache.size * 2),
        name="attend",
    )(*in_hbm(cache_len, *arrays, w_out))


def project_body(sides, *refs):
    blocks, weight = refs[:sides], refs[sides]
    mine, other, rows, total = refs[sides + 2 :]
    games = blocks[0].shape[0]
    depth, width = weight.shape
    for p in range(sides):
        rows[p * games : (p + 1) * games, :] = blocks[place_of(p, sides)][:, :depth]
    step = 512 if width % 512 == 0 else LANES
    for c in range(0, width, step):
        total[:, c : c + step] = jnp.dot(
            rows[...], weight[:, c : c + step], preferred_element_type=F32
        )
    odd = lax.axis_index("tensor") % 2
    half = width // 2
    mine[...] = total[:, columns(odd * half, half)]
    other[...] = total[:, columns((1 - odd) * half, half)].astype(BF16)


def project(sides, blocks, w_out, after):
    rows = blocks[0].shape[0] * sides
    depth, width = w_out.shape
    return pl.pallas_call(
        functools.partial(project_body, sides),
        in_specs=[VMEM] * (sides + 2),
        out_specs=[VMEM] * 2,
        out_shape=[
            jax.ShapeDtypeStruct((rows, width // 2), F32),
            jax.ShapeDtypeStruct((rows, width // 2), BF16),
        ],
        scratch_shapes=[pltpu.VMEM((rows, depth), BF16), pltpu.VMEM((rows, width), F32)],
        compiler_params=pltpu.CompilerParams(vmem_limit_bytes=SCOPE),
        cost_estimate=cost(2 * rows * depth * width, 2 * depth * width),
        name="project",
    )(*blocks, *in_vmem(w_out, after))


def add_body(mine, arrived, after, total, rounded):
    del after
    value = mine[...] + arrived[...].astype(F32)
    total[...] = value
    rounded[...] = value.astype(BF16)


def add(mine, arrived, after):
    return pl.pallas_call(
        add_body,
        in_specs=[VMEM, VMEM, VMEM],
        out_specs=[VMEM] * 2,
        out_shape=[
            jax.ShapeDtypeStruct(mine.shape, F32),
            jax.ShapeDtypeStruct(mine.shape, BF16),
        ],
        compiler_params=pltpu.CompilerParams(vmem_limit_bytes=SCOPE),
        name="add",
    )(mine, arrived, *in_vmem(after))


def stream_body(sides, depth, mine, arrived, *refs):
    blocks, out = refs[:sides], refs[-1]
    games = blocks[0].shape[0]
    width = out.shape[1]
    for p in range(sides):
        s = slice(p * games, (p + 1) * games)
        resid = blocks[place_of(p, sides)][:, depth : depth + width].astype(F32)
        out[s, :] = (resid + (mine[s] + arrived[s].astype(F32))).astype(BF16)


def stream_of(sides, depth, mine, arrived, blocks, after):
    return pl.pallas_call(
        functools.partial(stream_body, sides, depth),
        in_specs=[VMEM] * (sides + 3),
        out_specs=VMEM,
        out_shape=jax.ShapeDtypeStruct(mine.shape, BF16),
        compiler_params=pltpu.CompilerParams(vmem_limit_bytes=SCOPE),
        name="stream",
    )(mine, arrived, *blocks, *in_vmem(after))


def join_body(mine, arrived, after, out):
    del after
    width = mine.shape[1]
    odd = lax.axis_index("tensor") % 2
    out[:, columns(odd * width, width)] = mine[...]
    out[:, columns((1 - odd) * width, width)] = arrived[...]


def join(mine, arrived, after):
    rows, width = mine.shape
    return pl.pallas_call(
        join_body,
        in_specs=[VMEM] * 3,
        out_specs=VMEM,
        out_shape=jax.ShapeDtypeStruct((rows, 2 * width), BF16),
        compiler_params=pltpu.CompilerParams(vmem_limit_bytes=SCOPE),
        name="join",
    )(mine, arrived, *in_vmem(after))


def prefetch_body(first, count, per_slot, block, w_gate, w_up, w_down, after, *refs):
    del after
    outs, sems = refs[:-1], refs[-1]
    copies = []
    if block:
        start = lax.axis_index("tensor") * (w_down.shape[2] // lax.axis_size("tensor"))
        for i in range(w_down.shape[0]):
            copies.append(
                pltpu.make_async_copy(
                    w_down.at[i, :, columns(start, block)], outs[count].at[i], sems.at[count, i]
                )
            )
    for i, out in enumerate(outs[:count]):
        slot, block = divmod(first + i, per_slot)
        for half, weight in enumerate((w_gate, w_up)):
            copies.append(
                pltpu.make_async_copy(
                    weight.at[slot, :, pl.ds(block * FBLOCK, FBLOCK)],
                    out.at[half],
                    sems.at[i, half],
                )
            )
    for c in copies:
        c.start()
    for c in copies:
        c.wait()


def prefetch(first, count, weights, after, block=0):
    w_gate, _, w_down = weights
    slots, depth, hidden = w_gate.shape
    shapes = [(2, depth, FBLOCK)] * count + [(*w_down.shape[:2], block)] * bool(block)
    return list(
        pl.pallas_call(
            functools.partial(prefetch_body, first, count, hidden // FBLOCK, block),
            in_specs=[HBM] * 3 + [VMEM],
            out_specs=[VMEM] * len(shapes),
            out_shape=[pltpu.VMEM(s, BF16) for s in shapes],
            scratch_shapes=[pltpu.SemaphoreType.DMA((len(shapes), max(2, slots)))],
            compiler_params=pltpu.CompilerParams(vmem_limit_bytes=SCOPE),
            cost_estimate=cost(0, sum(2 * math.prod(s) for s in shapes)),
            name="prefetch",
        )(*in_hbm(*weights), after)
    )


def halves(value, gain, rows, where):
    count = value.shape[0]
    scaled = value.astype(F32) * gain.astype(F32)
    high = scaled.astype(BF16)
    rows[:count, where] = high
    rows[count:, where] = (scaled - high.astype(F32)).astype(BF16)


def fold(value):
    count = value.shape[0] // 2
    return value[:count] + value[count:]


def expand_body(sides, kept, split, ring, *refs):
    chunks, refs = refs[:sides], refs[sides:]
    blocks, refs = refs[:sides], refs[sides:]
    gain, router, w_gate, w_up = refs[:4]
    ready, refs = refs[4 : 4 + kept], refs[4 + kept :]
    inner, mine, stream, rows, router2, scale, norms, raw, buffer, sems = refs
    games = blocks[0].shape[0]
    count = games * sides
    width = chunks[0].shape[1]
    features = width * sides
    slots, _, hidden = w_gate.shape
    per_slot = hidden // FBLOCK
    streamed = slots * per_slot - kept
    side, tensor = lax.axis_index("side"), lax.axis_index("tensor")

    def copies(step):
        index = kept + step
        return [
            pltpu.make_async_copy(
                weight.at[index // per_slot, :, columns(index % per_slot * FBLOCK, FBLOCK)],
                buffer.at[step % ring, half],
                sems.at[step % ring, half],
            )
            for half, weight in enumerate((w_gate, w_up))
        ]

    for step in range(min(ring, streamed)):
        for c in copies(step):
            c.start()

    power = jnp.zeros((count, LANES), F32)
    experts = router.shape[0]
    for k in range(sides):
        base = jnp.bitwise_xor(side, k) * width
        flip = place_of(k, sides)
        for c in range(0, width, 512):
            value = jnp.concatenate(
                [
                    chunks[k][(p ^ flip) * games : (p ^ flip) * games + games, c : c + 512]
                    for p in range(sides)
                ],
                axis=0,
            )
            wide = value.astype(F32)
            for i in range(0, 512, LANES):
                power = power + wide[:, i : i + LANES] * wide[:, i : i + LANES]
            there = columns(base + c, 512)
            stream[:, there] = value[:games]
            halves(value, gain[:, there], rows, there)
            weight = router[:, there]
            top = weight.astype(BF16).astype(F32)
            router2[:, there] = jnp.concatenate([top, weight - top], axis=0).astype(BF16)
    norm = lax.rsqrt(jnp.sum(power, axis=-1, keepdims=True) / features + 1e-05)
    norms[...] = jnp.broadcast_to(norm, norms.shape)
    products = fold(
        lax.dot_general(
            rows[...], router2[...], (((1,), (1,)), ((), ())), preferred_element_type=F32
        )
    )
    logits = (products[:, :experts] + products[:, experts:]) * norm
    route = jnp.concatenate(
        [blocks[place_of(p, sides)][:, -LANES:] for p in range(sides)], axis=0
    ).astype(F32)
    lane = lax.broadcasted_iota(jnp.int32, route.shape, 1)
    ids = [jnp.sum(jnp.where(lane == j, route, 0.0), axis=-1, keepdims=True) for j in range(2)]
    number = lax.broadcasted_iota(jnp.int32, logits.shape, 1).astype(F32)
    chosen = [
        jnp.sum(jnp.where(number == ids[j], logits, 0.0), axis=-1, keepdims=True)
        for j in range(2)
    ]
    shares = [
        1.0 / (1.0 + jnp.exp(chosen[1] - chosen[0])),
        1.0 / (1.0 + jnp.exp(chosen[0] - chosen[1])),
    ]
    for i in range(slots):
        expert = ((side * slots + i) // split).astype(F32)
        weight = jnp.where(ids[0] == expert, shares[0], 0.0) + jnp.where(
            ids[1] == expert, shares[1], 0.0
        )
        scale[i] = jnp.broadcast_to(weight, (count, FBLOCK))
    mine[...] = stream[:, columns(tensor * mine.shape[1], mine.shape[1])]

    def products(weights, turn):
        for half in range(2):
            raw[turn % 2, half] = fold(
                jnp.dot(rows[...], weights[half], preferred_element_type=F32)
            )

    def finish(index, turn):
        gate = raw[turn % 2, 0] * norms[...]
        upward = raw[turn % 2, 1] * norms[...]
        value = gate / (1.0 + jnp.exp(-gate)) * upward * scale[index // per_slot]
        where = columns(index * FBLOCK, FBLOCK)
        high = value.astype(BF16)
        inner[:count, where] = high
        inner[count:, where] = (value - high.astype(F32)).astype(BF16)

    def from_ring(step, turn, before):
        for c in copies(step):
            c.wait()
        products(buffer.at[step % ring], turn)
        if before is not None:
            finish(before, turn + 1)

        @pl.when(step + ring < streamed)
        def _():
            for c in copies(step + ring):
                c.start()

    done, before = 0, None
    for index in range(kept + 1):
        until = streamed * (index + 1) // (kept + 1)
        if done < until:
            from_ring(jnp.int32(done), done + index, before)

            @pl.loop(done + 1, until)
            def _(step):
                from_ring(step, step + index, kept + step - 1)

            done, before = until, kept + until - 1
        if index < kept:
            products(ready[index], done + index)
            if before is not None:
                finish(before, done + index + 1)
            before = index
    finish(before, streamed + kept - 1)


def expand(sides, split, chunks, blocks, gain, router, w_gate, w_up, ready, own_width):
    games = blocks[0].shape[0]
    count = games * sides
    features = chunks[0].shape[1] * sides
    slots, _, hidden = w_gate.shape
    ring = 2
    arguments = [*chunks, *blocks, gain, router]
    return pl.pallas_call(
        functools.partial(expand_body, sides, len(ready), split, ring),
        in_specs=[VMEM] * len(arguments) + [HBM] * 2 + [VMEM] * len(ready),
        out_specs=[VMEM] * 2,
        out_shape=[
            jax.ShapeDtypeStruct((2 * count, slots * hidden), BF16),
            jax.ShapeDtypeStruct((games, own_width), BF16),
        ],
        scratch_shapes=[
            pltpu.VMEM((games, features), BF16),
            pltpu.VMEM((2 * count, features), BF16),
            pltpu.VMEM((2 * router.shape[0], features), BF16),
            pltpu.VMEM((slots, count, FBLOCK), F32),
            pltpu.VMEM((count, FBLOCK), F32),
            pltpu.VMEM((2, 2, count, FBLOCK), F32),
            pltpu.VMEM((ring, 2, features, FBLOCK), BF16),
            pltpu.SemaphoreType.DMA((ring, 2)),
        ],
        compiler_params=pltpu.CompilerParams(vmem_limit_bytes=16 * 2**20),
        cost_estimate=cost(8 * count * w_gate.size, 2 * w_gate.size * 2),
        name="expand",
    )(*arguments, *in_hbm(w_gate, w_up), *in_vmem(*ready))


def contract_body(tensors, ring, block, inner, first, w_down, keep, send, buffer, sems):
    slots, hidden, features = w_down.shape
    tensor = lax.axis_index("tensor")
    part = features // tensors
    per_part = part // block
    steps = features // block
    half = keep.shape[0]
    deep = ring // slots

    def copies(step):
        number = step // per_part
        bits = tensors.bit_length() - 1
        chunk = sum((number >> b) % 2 * 2 ** (bits - 1 - b) for b in range(bits))
        start = jnp.bitwise_xor(tensor, chunk) * part + step % per_part * block
        return [
            pltpu.make_async_copy(
                w_down.at[slot, :, columns(start, block)],
                buffer.at[step % deep, slot],
                sems.at[step % deep, slot],
            )
            for slot in range(slots)
        ]

    for step in range(1, min(deep + 1, steps)):
        for c in copies(step):
            c.start()

    def run(step, more, weights):
        total = None
        for slot in range(slots):
            value = jnp.dot(
                inner[:, slot * hidden : (slot + 1) * hidden],
                weights[slot],
                preferred_element_type=F32,
            )
            total = value if total is None else total + value
        total = fold(total)
        where = columns(step * block, block)
        keep[:, where] = total[:half]
        send[:, where] = total[half:].astype(BF16)
        if more:
            for c in copies(step + deep):
                c.start()

    def from_ring(step, more):
        for c in copies(step):
            c.wait()
        run(step, more, buffer.at[step % deep])

    run(0, False, first)
    edge = max(1, steps - deep)
    pl.loop(1, edge)(lambda step: from_ring(step, True))
    for step in range(edge, steps):
        from_ring(step, False)


def contract(tensors, block, inner, first, w_down):
    count = inner.shape[0] // 2
    slots, hidden, features = w_down.shape
    ring = 3 * slots
    return pl.pallas_call(
        functools.partial(contract_body, tensors, ring, block),
        in_specs=[VMEM, VMEM, HBM],
        out_specs=[VMEM, VMEM],
        out_shape=[
            jax.ShapeDtypeStruct((count // 2, features), F32),
            jax.ShapeDtypeStruct((count // 2, features), BF16),
        ],
        scratch_shapes=[
            pltpu.VMEM((ring // slots, slots, hidden, block), BF16),
            pltpu.SemaphoreType.DMA((ring // slots, slots)),
        ],
        compiler_params=pltpu.CompilerParams(vmem_limit_bytes=16 * 2**20),
        cost_estimate=cost(4 * count * w_down.size, 2 * w_down.size),
        name="contract",
    )(inner, *in_vmem(first), *in_hbm(w_down))


def halve_body(keep, arrived, low_here, low_there, high_here, high_there):
    total = keep[...] + arrived[...].astype(F32)
    rows, width = low_here.shape
    low_here[...] = total[:rows, :width]
    low_there[...] = total[:rows, width:]
    high_here[...] = total[rows:, :width].astype(BF16)
    high_there[...] = total[rows:, width:].astype(BF16)


def halve(keep, arrived):
    rows, width = keep.shape
    return pl.pallas_call(
        halve_body,
        in_specs=[VMEM] * 2,
        out_specs=[VMEM] * 4,
        out_shape=[jax.ShapeDtypeStruct((rows // 2, width // 2), t) for t in (F32, F32, BF16, BF16)],
        compiler_params=pltpu.CompilerParams(vmem_limit_bytes=SCOPE),
        name="halve",
    )(keep, arrived)


def total_body(low, arrived, out):
    out[...] = (low[...] + arrived[...].astype(F32)).astype(BF16)


def total_of(low, arrived):
    return pl.pallas_call(
        total_body,
        in_specs=[VMEM] * 2,
        out_specs=VMEM,
        out_shape=jax.ShapeDtypeStruct(low.shape, BF16),
        compiler_params=pltpu.CompilerParams(vmem_limit_bytes=SCOPE),
        name="total",
    )(low, arrived)


def split_body(*refs):
    parts, (keep, send) = refs[:-2], refs[-2:]
    value = parts[0][...]
    for part in parts[1:]:
        value = value + part[...].astype(F32)
    width = keep.shape[1]
    keep[...] = value[:, :width]
    send[...] = value[:, width:].astype(BF16)


def split_columns(*parts):
    rows, width = parts[0].shape
    return pl.pallas_call(
        split_body,
        in_specs=[VMEM] * len(parts),
        out_specs=[VMEM] * 2,
        out_shape=[jax.ShapeDtypeStruct((rows, width // 2), t) for t in (F32, BF16)],
        compiler_params=pltpu.CompilerParams(vmem_limit_bytes=SCOPE),
        name="split",
    )(*parts)


def last_body(*refs):
    stream, parts, out = refs[0], refs[1:-1], refs[-1]
    total = parts[0][...]
    for part in parts[1:]:
        total = total + part[...].astype(F32)
    out[...] = (stream[...].astype(F32) + total).astype(BF16)


def last(stream, parts):
    return pl.pallas_call(
        last_body,
        in_specs=[VMEM] * (1 + len(parts)),
        out_specs=VMEM,
        out_shape=jax.ShapeDtypeStruct(stream.shape, BF16),
        compiler_params=pltpu.CompilerParams(vmem_limit_bytes=SCOPE),
        name="last",
    )(stream, *parts)


def shards_kernels(
    query,
    new_key,
    new_value,
    key_cache,
    value_cache,
    cache_len,
    resid,
    w_out,
    rms_gain,
    w_router,
    route_ids,
    w_gate,
    w_up,
    w_down,
):
    sides, tensors = lax.axis_size("side"), lax.axis_size("tensor")
    features = resid.shape[1]
    depth = query.shape[1]
    extra = features // sides // 2
    slots, _, hidden = w_gate.shape
    held = [1, 1, 1, 1, 1]
    weights = (w_gate, w_up, w_down)
    *blocks, w_here = attend(
        sides,
        extra,
        query,
        new_key,
        new_value,
        key_cache,
        value_cache,
        cache_len,
        resid,
        route_ids,
        w_out,
    )
    ready = prefetch(0, held[0], weights, blocks[0])
    blocks = [blocks[0]] + [swap(blocks[k], "side", sides, k) for k in range(1, sides)]
    mine, other = project(sides, blocks, w_here, ready[-1])
    ready += prefetch(len(ready), held[1], weights, other)
    mine, other = add(mine, swap(other, "tensor", tensors, 1), ready[-1])
    ready += prefetch(len(ready), held[2], weights, other)
    step = 2
    while step < tensors // 2:
        mine, other = add(mine, swap(other, "tensor", tensors, step), ready[-1])
        step *= 2
    stream = stream_of(sides, depth, mine, swap(other, "tensor", tensors, step), blocks, ready[-1])
    ready += prefetch(len(ready), held[3], weights, stream)
    own = join(stream, swap(stream, "tensor", tensors, 1), ready[-1])
    part = features // tensors
    block = 512 if part % 512 == 0 else LANES
    *more, down = prefetch(len(ready), held[4], weights, own, block)
    ready += more
    across = swap(own, "side", sides, 2)
    beside = swap(own, "side", sides, 1)
    across, down = lax.optimization_barrier((across, down))
    chunks = [own, beside, across, swap(across, "side", sides, 1)]
    inner, mine = expand(
        sides,
        slots * sides // w_router.shape[1],
        chunks,
        blocks,
        rms_gain.reshape(1, features),
        w_router.T,
        w_gate,
        w_up,
        ready,
        part,
    )
    keep, send = contract(tensors, block, inner, down, w_down)
    low_here, low_there, high_here, high_there = halve(keep, swap(send, "side", sides, 1))
    there = total_of(low_there, swap(high_there, "side", sides, 2))
    parts = [low_here, swap(high_here, "side", sides, 2), swap(there, "tensor", tensors, 1)]
    mask = 2
    while mask < tensors:
        keep, send = split_columns(*parts)
        parts = [keep, swap(send, "tensor", tensors, mask)]
        mask *= 2
    return last(mine, parts)


def attend_local(query, new_key, new_value, key_cache, value_cache, cache_len):
    count = query.shape[0]
    positions = key_cache.shape[1]
    kv_local = key_cache.shape[2] // HEAD_DIM
    repeat = query.shape[1] // (kv_local * HEAD_DIM)
    queries = query.reshape(count, kv_local, repeat, HEAD_DIM)
    cached_keys = key_cache.reshape(count, positions, kv_local, HEAD_DIM)
    cached_values = value_cache.reshape(count, positions, kv_local, HEAD_DIM)
    scale = 1.0 / HEAD_DIM**0.5
    scores = (
        jnp.einsum("gkrd,gpkd->gkrp", queries, cached_keys, preferred_element_type=jnp.float32)
        * scale
    )
    own_key = new_key.reshape(count, kv_local, HEAD_DIM)
    own_score = (
        jnp.einsum("gkrd,gkd->gkr", queries, own_key, preferred_element_type=jnp.float32) * scale
    )
    valid = jnp.arange(positions, dtype=jnp.int32)[None, :] < cache_len[:, None]
    scores = jnp.where(valid[:, None, None, :], scores, -jnp.inf)
    highest = jnp.maximum(jnp.max(scores, axis=-1), own_score)
    cached_weight = jnp.exp(scores - highest[..., None])
    own_weight = jnp.exp(own_score - highest)
    total = jnp.sum(cached_weight, axis=-1) + own_weight
    cached_weight = (cached_weight / total[..., None]).astype(jnp.bfloat16)
    own_weight = (own_weight / total).astype(jnp.bfloat16)
    mixed = jnp.einsum(
        "gkrp,gpkd->gkrd", cached_weight, cached_values, preferred_element_type=jnp.float32
    )
    own_value = new_value.reshape(count, kv_local, 1, HEAD_DIM).astype(jnp.float32)
    mixed = mixed + own_weight.astype(jnp.float32)[..., None] * own_value
    return mixed.reshape(count, kv_local * repeat * HEAD_DIM).astype(jnp.bfloat16)


def shards(
    query,
    new_key,
    new_value,
    key_cache,
    value_cache,
    cache_len,
    resid,
    w_out,
    rms_gain,
    w_router,
    route_ids,
    w_gate,
    w_up,
    w_down,
):
    attended = attend_local(query, new_key, new_value, key_cache, value_cache, cache_len)
    column_part = jnp.dot(
        lax.all_gather(attended, "side", axis=0, tiled=True),
        w_out,
        preferred_element_type=jnp.float32,
    )
    partial_out = lax.all_to_all(column_part, "side", split_axis=0, concat_axis=1, tiled=True)
    attn_out = lax.psum(partial_out, "tensor")
    stream = (resid.astype(jnp.float32) + attn_out).astype(jnp.bfloat16)
    wide = stream.astype(jnp.float32)
    power = jnp.mean(wide * wide, axis=-1, keepdims=True)
    normed = wide * lax.rsqrt(power + 1e-05) * rms_gain.astype(jnp.float32)
    logits = jnp.dot(normed, w_router, precision=lax.Precision.HIGHEST)
    experts = w_router.shape[1]
    picked = route_ids[:, :, None] == jnp.arange(experts, dtype=jnp.int32)[None, None, :]
    chosen = jnp.sum(jnp.where(picked, logits[:, None, :], 0.0), axis=-1)
    first = 1.0 / (1.0 + jnp.exp(chosen[:, 1] - chosen[:, 0]))
    second = 1.0 / (1.0 + jnp.exp(chosen[:, 0] - chosen[:, 1]))
    pair = jnp.stack([first, second], axis=1)
    weight = jnp.sum(jnp.where(picked, pair[:, :, None], 0.0), axis=1)
    rows = normed.astype(jnp.bfloat16)
    member = jnp.any(picked, axis=1).astype(jnp.int32)
    order_rank = jnp.cumsum(member, axis=0) - member
    capacity = CAP
    placing = (order_rank.T[:, None, :] == jnp.arange(capacity, dtype=jnp.int32)[None, :, None]) & (
        member.T[:, None, :] == 1
    )
    packed = jnp.einsum(
        "ecg,gd->ecd", placing.astype(jnp.bfloat16), rows, preferred_element_type=jnp.float32
    ).astype(jnp.bfloat16)
    side_count = lax.axis_size("side")
    slot_total = max(side_count, experts)
    split_count = slot_total // experts
    slot_local = slot_total // side_count
    width = rows.shape[1]
    packed = jnp.repeat(packed, split_count, axis=0).reshape(
        side_count, slot_local, capacity, width
    )
    arrived = lax.all_to_all(packed, "side", split_axis=0, concat_axis=0, tiled=True)
    gate = jnp.einsum("sjcd,jdf->sjcf", arrived, w_gate, preferred_element_type=jnp.float32)
    upward = jnp.einsum("sjcd,jdf->sjcf", arrived, w_up, preferred_element_type=jnp.float32)
    inner = (jax.nn.silu(gate) * upward).astype(jnp.bfloat16)
    expert_part = jnp.einsum("sjcf,jfd->sjcd", inner, w_down, preferred_element_type=jnp.float32)
    scaled_place = placing.astype(jnp.float32) * weight.T[:, None, :]
    returned = lax.all_to_all(expert_part, "side", split_axis=0, concat_axis=0, tiled=True)
    features = returned.shape[3]
    merged = jnp.sum(returned.reshape(experts, split_count, capacity, features), axis=1)
    moe = lax.psum_scatter(
        jnp.einsum("ecg,ecf->gf", scaled_place, merged, precision=lax.Precision.HIGHEST),
        "tensor",
        scatter_dimension=1,
        tiled=True,
    )
    columns = moe.shape[1]
    local_stream = lax.dynamic_slice_in_dim(wide, lax.axis_index("tensor") * columns, columns, 1)
    return (local_stream + moe).astype(jnp.bfloat16)


def tiles(mesh, sides=4):
    side, tensor = mesh.shape["side"], mesh.shape["tensor"]
    return side == sides and tensor >= 4 and tensor & (tensor - 1) == 0


def solution(mesh):
    return jax.shard_map(
        shards_kernels if tiles(mesh) else shards,
        mesh=mesh,
        in_specs=(
            P(("groups", "side"), "tensor"),
            P(("groups", "side"), "tensor"),
            P(("groups", "side"), "tensor"),
            P(("groups", "side"), None, "tensor"),
            P(("groups", "side"), None, "tensor"),
            P(("groups", "side")),
            P(("groups", "side"), None),
            P("tensor", "side"),
            P(),
            P(),
            P(("groups", "side"), None),
            P("side", None, "tensor"),
            P("side", None, "tensor"),
            P("side", "tensor", None),
        ),
        out_specs=P(("groups", "side"), "tensor"),
        check_vma=False,
    )
```

```python
import functools
import math

import jax
import jax.numpy as jnp
from jax import lax
from jax.experimental import pallas as pl
from jax.experimental.pallas import tpu as pltpu
from jax.sharding import PartitionSpec as P

HEAD_DIM = 128
CAP = 12
LANES = 128
FBLOCK = 256
BF16 = jnp.bfloat16
F32 = jnp.float32
SCOPE = 8 * 2**20
VMEM = pl.BlockSpec(memory_space=pltpu.VMEM)
ANY = pl.BlockSpec(memory_space=pl.ANY)
HBM = pl.BlockSpec(memory_space=pltpu.HBM)


def cost(flops, moved):
    return pl.CostEstimate(flops=int(flops), bytes_accessed=int(moved), transcendentals=0)


def place_of(position, count):
    bits = count.bit_length() - 1
    return sum(((position >> b) & 1) << (bits - 1 - b) for b in range(bits))


def swap(value, axis, count, mask):
    return lax.ppermute(value, axis, [(i, i ^ mask) for i in range(count)])


def in_hbm(*arrays):
    return [pltpu.with_memory_space_constraint(a, pltpu.HBM) for a in arrays]


def in_vmem(*arrays):
    return [pltpu.with_memory_space_constraint(a, pltpu.VMEM) for a in arrays]


def columns(start, size):
    return pl.ds(pl.multiple_of(start, LANES), size)


def attend_body(
    sides,
    block,
    length_at,
    query_at,
    new_key_at,
    new_value_at,
    keys_at,
    values_at,
    resid_at,
    route_at,
    w_out_at,
    *rest,
):
    outs, w_out, rest = rest[:sides], rest[sides], rest[sides + 1 :]
    query, new_key, new_value, keys, values, resid, route, sems, rest = *rest[:8], rest[8:]
    length, spread, mixed, score, own_score, key32, value32 = rest
    games, width = query.shape
    heads = width // HEAD_DIM
    padded = spread.shape[1]
    wide = new_key.shape[1]
    repeat = heads * HEAD_DIM // wide
    scale = 1.0 / HEAD_DIM**0.5
    steps = games // block

    def copy(source, target, sem):
        return pltpu.make_async_copy(source, target, sems.at[sem])

    small = [
        copy(source, target, i)
        for i, (source, target) in enumerate(
            (
                (query_at, query),
                (new_key_at, new_key),
                (new_value_at, new_value),
                (route_at, route),
                (resid_at, resid),
            )
        )
    ]
    caches = [
        [
            copy(source.at[pl.ds(i * block, block)], target.at[pl.ds(i * block, block)], sem + i)
            for i in range(steps)
        ]
        for source, target, sem in ((keys_at, keys, 5), (values_at, values, 5 + steps))
    ]
    after = copy(w_out_at, w_out, 5 + 2 * steps)
    lengths = copy(length_at, length, 6 + 2 * steps)
    for c in [lengths] + small[:4] + caches[0] + caches[1] + small[4:] + [after]:
        c.start()
    spread[...] = jnp.zeros_like(spread)
    for c in [lengths] + small[:4]:
        c.wait()
    for h in range(heads):
        lane = h // repeat * HEAD_DIM
        spread[:, h, lane : lane + HEAD_DIM] = query[
            :, h * HEAD_DIM : (h + 1) * HEAD_DIM
        ].astype(F32)
    key32[...] = new_key[...].astype(F32)
    value32[...] = new_value[...].astype(F32)
    for game in range(games):
        if game % block == 0:
            caches[0][game // block].wait()
        q = spread[game]
        s = slice(game * padded, (game + 1) * padded)
        value = (
            lax.dot_general(
                q.astype(BF16), keys[game], (((1,), (1,)), ((), ())), preferred_element_type=F32
            )
            * scale
        )
        at = lax.broadcasted_iota(jnp.int32, value.shape, 1)
        score[s] = jnp.where(at < length[game], value, -jnp.inf)
        own = jnp.sum(q * key32[game : game + 1, :], axis=-1, keepdims=True) * scale
        own_score[s] = jnp.broadcast_to(own, (padded, LANES))
    for i in range(steps):
        s = slice(i * block * padded, (i + 1) * block * padded)
        own = own_score[s][:, :1]
        value = score[s]
        top = jnp.maximum(jnp.max(value, axis=-1, keepdims=True), own)
        e = jnp.exp(value - top)
        own_e = jnp.exp(own - top)
        total = jnp.sum(e, axis=-1, keepdims=True) + own_e
        score[s] = e / total
        own_score[s] = jnp.broadcast_to(
            (own_e / total).astype(BF16).astype(F32), (block * padded, LANES)
        )
        caches[1][i].wait()
        for game in range(i * block, (i + 1) * block):
            s = slice(game * padded, (game + 1) * padded)
            mixed[game] = (
                jnp.dot(score[s].astype(BF16), values[game], preferred_element_type=F32)
                + own_score[s][:, :1] * value32[game : game + 1, :]
            )
    small[4].wait()
    side, tensor = lax.axis_index("side"), lax.axis_index("tensor")
    for h in range(heads):
        lane = h // repeat * HEAD_DIM
        part = mixed[:, h, lane : lane + HEAD_DIM].astype(BF16)
        for out in outs:
            out[:, h * HEAD_DIM : (h + 1) * HEAD_DIM] = part
    extra = outs[0].shape[1] - width - LANES
    row = lax.broadcasted_iota(jnp.int32, (games, games), 0)
    diagonal = row == lax.broadcasted_iota(jnp.int32, (games, games), 1)
    lane = lax.broadcasted_iota(jnp.int32, (games, LANES), 1)
    routes = jnp.zeros((games, LANES), F32)
    for j in range(route.shape[0]):
        ids = jnp.broadcast_to(route[j : j + 1, :].astype(F32), (games, games))
        column = jnp.sum(jnp.where(diagonal, ids, 0.0), axis=-1, keepdims=True)
        routes = jnp.where(lane == j, column, routes)
    features = resid.shape[1] // sides
    for k, out in enumerate(outs):
        start = jnp.bitwise_xor(side, k) * features + tensor % 2 * extra
        out[:, width : width + extra] = resid[:, columns(start, extra)]
        out[:, width + extra :] = routes.astype(BF16)
    after.wait()


def attend(
    sides, extra, query, new_key, new_value, key_cache, value_cache, cache_len, resid, route_ids, w_out
):
    games, width = query.shape
    positions, wide = key_cache.shape[1:]
    block = 4
    heads = -(-(width // HEAD_DIM) // 16) * 16
    out = jax.ShapeDtypeStruct((games, width + extra + LANES), BF16)
    routes = route_ids.T
    arrays = [query, new_key, new_value, key_cache, value_cache, resid, routes]
    return pl.pallas_call(
        functools.partial(attend_body, sides, block),
        in_specs=[HBM] * (len(arrays) + 2),
        out_specs=[VMEM] * (sides + 1),
        out_shape=[out] * sides + [pltpu.VMEM(w_out.shape, BF16)],
        scratch_shapes=[pltpu.VMEM(a.shape, a.dtype) for a in arrays]
        + [
            pltpu.SemaphoreType.DMA((7 + 2 * (games // block),)),
            pltpu.SMEM(cache_len.shape, jnp.int32),
            pltpu.VMEM((games, heads, wide), F32),
            pltpu.VMEM((games, heads, wide), F32),
            pltpu.VMEM((games * heads, positions), F32),
            pltpu.VMEM((games * heads, LANES), F32),
            pltpu.VMEM((games, wide), F32),
            pltpu.VMEM((games, wide), F32),
        ],
        compiler_params=pltpu.CompilerParams(vmem_limit_bytes=SCOPE),
        cost_estimate=cost(4 * games * heads * positions * wide, 2 * key_cache.size * 2),
        name="attend",
    )(*in_hbm(cache_len, *arrays, w_out))


def project_body(sides, *refs):
    blocks, weight = refs[:sides], refs[sides]
    mine, other, rows, total = refs[sides + 2 :]
    games = blocks[0].shape[0]
    depth, width = weight.shape
    for p in range(sides):
        rows[p * games : (p + 1) * games, :] = blocks[place_of(p, sides)][:, :depth]
    step = 512 if width % 512 == 0 else LANES
    for c in range(0, width, step):
        total[:, c : c + step] = jnp.dot(
            rows[...], weight[:, c : c + step], preferred_element_type=F32
        )
    odd = lax.axis_index("tensor") % 2
    half = width // 2
    mine[...] = total[:, columns(odd * half, half)]
    other[...] = total[:, columns((1 - odd) * half, half)].astype(BF16)


def project(sides, blocks, w_out, after):
    rows = blocks[0].shape[0] * sides
    depth, width = w_out.shape
    return pl.pallas_call(
        functools.partial(project_body, sides),
        in_specs=[VMEM] * (sides + 2),
        out_specs=[VMEM] * 2,
        out_shape=[
            jax.ShapeDtypeStruct((rows, width // 2), F32),
            jax.ShapeDtypeStruct((rows, width // 2), BF16),
        ],
        scratch_shapes=[pltpu.VMEM((rows, depth), BF16), pltpu.VMEM((rows, width), F32)],
        compiler_params=pltpu.CompilerParams(vmem_limit_bytes=SCOPE),
        cost_estimate=cost(2 * rows * depth * width, 2 * depth * width),
        name="project",
    )(*blocks, *in_vmem(w_out, after))


def add_body(mine, arrived, after, total, rounded):
    del after
    value = mine[...] + arrived[...].astype(F32)
    total[...] = value
    rounded[...] = value.astype(BF16)


def add(mine, arrived, after):
    return pl.pallas_call(
        add_body,
        in_specs=[VMEM, VMEM, VMEM],
        out_specs=[VMEM] * 2,
        out_shape=[
            jax.ShapeDtypeStruct(mine.shape, F32),
            jax.ShapeDtypeStruct(mine.shape, BF16),
        ],
        compiler_params=pltpu.CompilerParams(vmem_limit_bytes=SCOPE),
        name="add",
    )(mine, arrived, *in_vmem(after))


def stream_body(sides, depth, mine, arrived, *refs):
    blocks, out = refs[:sides], refs[-1]
    games = blocks[0].shape[0]
    width = out.shape[1]
    for p in range(sides):
        s = slice(p * games, (p + 1) * games)
        resid = blocks[place_of(p, sides)][:, depth : depth + width].astype(F32)
        out[s, :] = (resid + (mine[s] + arrived[s].astype(F32))).astype(BF16)


def stream_of(sides, depth, mine, arrived, blocks, after):
    return pl.pallas_call(
        functools.partial(stream_body, sides, depth),
        in_specs=[VMEM] * (sides + 3),
        out_specs=VMEM,
        out_shape=jax.ShapeDtypeStruct(mine.shape, BF16),
        compiler_params=pltpu.CompilerParams(vmem_limit_bytes=SCOPE),
        name="stream",
    )(mine, arrived, *blocks, *in_vmem(after))


def join_body(mine, arrived, after, out):
    del after
    width = mine.shape[1]
    odd = lax.axis_index("tensor") % 2
    out[:, columns(odd * width, width)] = mine[...]
    out[:, columns((1 - odd) * width, width)] = arrived[...]


def join(mine, arrived, after):
    rows, width = mine.shape
    return pl.pallas_call(
        join_body,
        in_specs=[VMEM] * 3,
        out_specs=VMEM,
        out_shape=jax.ShapeDtypeStruct((rows, 2 * width), BF16),
        compiler_params=pltpu.CompilerParams(vmem_limit_bytes=SCOPE),
        name="join",
    )(mine, arrived, *in_vmem(after))


def prefetch_body(first, count, per_slot, block, number, w_gate, w_up, w_down, after, *refs):
    del after
    outs, sems = refs[:-1], refs[-1]
    copies = []
    if block:
        start = lax.axis_index("tensor") * (w_down.shape[2] // lax.axis_size("tensor"))
        start = start + number * block
        for i in range(w_down.shape[0]):
            copies.append(
                pltpu.make_async_copy(
                    w_down.at[i, :, columns(start, block)], outs[count].at[i], sems.at[count, i]
                )
            )
    for i, out in enumerate(outs[:count]):
        slot, block = divmod(first + i, per_slot)
        for half, weight in enumerate((w_gate, w_up)):
            copies.append(
                pltpu.make_async_copy(
                    weight.at[slot, :, pl.ds(block * FBLOCK, FBLOCK)],
                    out.at[half],
                    sems.at[i, half],
                )
            )
    for c in copies:
        c.start()
    for c in copies:
        c.wait()


def prefetch(first, count, weights, after, block=0, number=0):
    w_gate, _, w_down = weights
    slots, depth, hidden = w_gate.shape
    shapes = [(2, depth, FBLOCK)] * count + [(*w_down.shape[:2], block)] * bool(block)
    return list(
        pl.pallas_call(
            functools.partial(prefetch_body, first, count, hidden // FBLOCK, block, number),
            in_specs=[HBM] * 3 + [VMEM],
            out_specs=[VMEM] * len(shapes),
            out_shape=[pltpu.VMEM(s, BF16) for s in shapes],
            scratch_shapes=[pltpu.SemaphoreType.DMA((len(shapes), max(2, slots)))],
            compiler_params=pltpu.CompilerParams(vmem_limit_bytes=SCOPE),
            cost_estimate=cost(0, sum(2 * math.prod(s) for s in shapes)),
            name="prefetch",
        )(*in_hbm(*weights), after)
    )


def halves(value, gain, rows, where):
    count = value.shape[0]
    scaled = value.astype(F32) * gain.astype(F32)
    high = scaled.astype(BF16)
    rows[:count, where] = high
    rows[count:, where] = (scaled - high.astype(F32)).astype(BF16)


def fold(value):
    count = value.shape[0] // 2
    return value[:count] + value[count:]


def expand_body(sides, kept, split, ring, *refs):
    chunks, refs = refs[:sides], refs[sides:]
    blocks, refs = refs[:sides], refs[sides:]
    gain, router, w_gate, w_up = refs[:4]
    ready, refs = refs[4 : 4 + kept], refs[4 + kept :]
    inner, mine, stream, rows, router2, scale, norms, raw, buffer, sems = refs
    games = blocks[0].shape[0]
    count = games * sides
    width = chunks[0].shape[1]
    features = width * sides
    slots, _, hidden = w_gate.shape
    per_slot = hidden // FBLOCK
    streamed = slots * per_slot - kept
    side, tensor = lax.axis_index("side"), lax.axis_index("tensor")

    def copies(step):
        index = kept + step
        return [
            pltpu.make_async_copy(
                weight.at[index // per_slot, :, columns(index % per_slot * FBLOCK, FBLOCK)],
                buffer.at[step % ring, half],
                sems.at[step % ring, half],
            )
            for half, weight in enumerate((w_gate, w_up))
        ]

    for step in range(min(ring, streamed)):
        for c in copies(step):
            c.start()

    power = jnp.zeros((count, LANES), F32)
    experts = router.shape[0]
    for k in range(sides):
        base = jnp.bitwise_xor(side, k) * width
        flip = place_of(k, sides)
        for c in range(0, width, 512):
            value = jnp.concatenate(
                [
                    chunks[k][(p ^ flip) * games : (p ^ flip) * games + games, c : c + 512]
                    for p in range(sides)
                ],
                axis=0,
            )
            wide = value.astype(F32)
            for i in range(0, 512, LANES):
                power = power + wide[:, i : i + LANES] * wide[:, i : i + LANES]
            there = columns(base + c, 512)
            stream[:, there] = value[:games]
            halves(value, gain[:, there], rows, there)
            weight = router[:, there]
            top = weight.astype(BF16).astype(F32)
            router2[:, there] = jnp.concatenate([top, weight - top], axis=0).astype(BF16)
    norm = lax.rsqrt(jnp.sum(power, axis=-1, keepdims=True) / features + 1e-05)
    norms[...] = jnp.broadcast_to(norm, norms.shape)
    products = fold(
        lax.dot_general(
            rows[...], router2[...], (((1,), (1,)), ((), ())), preferred_element_type=F32
        )
    )
    logits = (products[:, :experts] + products[:, experts:]) * norm
    route = jnp.concatenate(
        [blocks[place_of(p, sides)][:, -LANES:] for p in range(sides)], axis=0
    ).astype(F32)
    lane = lax.broadcasted_iota(jnp.int32, route.shape, 1)
    ids = [jnp.sum(jnp.where(lane == j, route, 0.0), axis=-1, keepdims=True) for j in range(2)]
    number = lax.broadcasted_iota(jnp.int32, logits.shape, 1).astype(F32)
    chosen = [
        jnp.sum(jnp.where(number == ids[j], logits, 0.0), axis=-1, keepdims=True)
        for j in range(2)
    ]
    shares = [
        1.0 / (1.0 + jnp.exp(chosen[1] - chosen[0])),
        1.0 / (1.0 + jnp.exp(chosen[0] - chosen[1])),
    ]
    for i in range(slots):
        expert = ((side * slots + i) // split).astype(F32)
        weight = jnp.where(ids[0] == expert, shares[0], 0.0) + jnp.where(
            ids[1] == expert, shares[1], 0.0
        )
        scale[i] = jnp.broadcast_to(weight, (count, FBLOCK))
    mine[...] = stream[:, columns(tensor * mine.shape[1], mine.shape[1])]

    def products(weights, turn):
        for half in range(2):
            raw[turn % 2, half] = fold(
                jnp.dot(rows[...], weights[half], preferred_element_type=F32)
            )

    def finish(index, turn):
        gate = raw[turn % 2, 0] * norms[...]
        upward = raw[turn % 2, 1] * norms[...]
        value = gate / (1.0 + jnp.exp(-gate)) * upward * scale[index // per_slot]
        where = columns(index * FBLOCK, FBLOCK)
        high = value.astype(BF16)
        inner[:count, where] = high
        inner[count:, where] = (value - high.astype(F32)).astype(BF16)

    def from_ring(step, turn, before):
        for c in copies(step):
            c.wait()
        products(buffer.at[step % ring], turn)
        if before is not None:
            finish(before, turn + 1)

        @pl.when(step + ring < streamed)
        def _():
            for c in copies(step + ring):
                c.start()

    done, before = 0, None
    for index in range(kept + 1):
        until = streamed * (index + 1) // (kept + 1)
        if done < until:
            from_ring(jnp.int32(done), done + index, before)

            @pl.loop(done + 1, until)
            def _(step):
                from_ring(step, step + index, kept + step - 1)

            done, before = until, kept + until - 1
        if index < kept:
            products(ready[index], done + index)
            if before is not None:
                finish(before, done + index + 1)
            before = index
    finish(before, streamed + kept - 1)


def expand(sides, split, chunks, blocks, gain, router, w_gate, w_up, ready, own_width):
    games = blocks[0].shape[0]
    count = games * sides
    features = chunks[0].shape[1] * sides
    slots, _, hidden = w_gate.shape
    ring = 2
    arguments = [*chunks, *blocks, gain, router]
    return pl.pallas_call(
        functools.partial(expand_body, sides, len(ready), split, ring),
        in_specs=[VMEM] * len(arguments) + [HBM] * 2 + [VMEM] * len(ready),
        out_specs=[VMEM] * 2,
        out_shape=[
            jax.ShapeDtypeStruct((2 * count, slots * hidden), BF16),
            jax.ShapeDtypeStruct((games, own_width), BF16),
        ],
        scratch_shapes=[
            pltpu.VMEM((games, features), BF16),
            pltpu.VMEM((2 * count, features), BF16),
            pltpu.VMEM((2 * router.shape[0], features), BF16),
            pltpu.VMEM((slots, count, FBLOCK), F32),
            pltpu.VMEM((count, FBLOCK), F32),
            pltpu.VMEM((2, 2, count, FBLOCK), F32),
            pltpu.VMEM((ring, 2, features, FBLOCK), BF16),
            pltpu.SemaphoreType.DMA((ring, 2)),
        ],
        compiler_params=pltpu.CompilerParams(vmem_limit_bytes=16 * 2**20),
        cost_estimate=cost(8 * count * w_gate.size, 2 * w_gate.size * 2),
        name="expand",
    )(*arguments, *in_hbm(w_gate, w_up), *in_vmem(*ready))


def contract_body(tensors, ring, block, kept, inner, *refs):
    ready, (w_down, keep, send, buffer, sems) = refs[:kept], refs[kept:]
    slots, hidden, features = w_down.shape
    tensor = lax.axis_index("tensor")
    part = features // tensors
    per_part = part // block
    steps = features // block
    half = keep.shape[0]
    deep = ring // slots

    def copies(step):
        start = jnp.bitwise_xor(tensor, step // per_part) * part + step % per_part * block
        return [
            pltpu.make_async_copy(
                w_down.at[slot, :, columns(start, block)],
                buffer.at[step % deep, slot],
                sems.at[step % deep, slot],
            )
            for slot in range(slots)
        ]

    for step in range(kept, min(deep + kept, steps)):
        for c in copies(step):
            c.start()

    def run(step, more, weights, arriving=()):
        total = None
        for c in arriving:
            c.wait()
        for slot in range(slots):
            value = jnp.dot(
                inner[:, slot * hidden : (slot + 1) * hidden],
                weights[slot],
                preferred_element_type=F32,
            )
            total = value if total is None else total + value
        total = fold(total)
        where = columns(step * block, block)
        keep[:, where] = total[:half]
        send[:, where] = total[half:].astype(BF16)
        if more:
            for c in copies(step + deep):
                c.start()

    def from_ring(step, more):
        run(step, more, buffer.at[step % deep], copies(step))

    for step, weights in enumerate(ready):
        run(step, False, weights)
    edge = max(kept, steps - deep)
    pl.loop(kept, edge)(lambda step: from_ring(step, True))
    for step in range(edge, steps):
        from_ring(step, False)


def contract(tensors, block, inner, ready, w_down):
    count = inner.shape[0] // 2
    slots, hidden, features = w_down.shape
    ring = 3 * slots
    return pl.pallas_call(
        functools.partial(contract_body, tensors, ring, block, len(ready)),
        in_specs=[VMEM] * (1 + len(ready)) + [HBM],
        out_specs=[VMEM, VMEM],
        out_shape=[
            jax.ShapeDtypeStruct((count // 2, features), F32),
            jax.ShapeDtypeStruct((count // 2, features), BF16),
        ],
        scratch_shapes=[
            pltpu.VMEM((ring // slots, slots, hidden, block), BF16),
            pltpu.SemaphoreType.DMA((ring // slots, slots)),
        ],
        compiler_params=pltpu.CompilerParams(vmem_limit_bytes=16 * 2**20),
        cost_estimate=cost(4 * count * w_down.size, 2 * w_down.size),
        name="contract",
    )(inner, *in_vmem(*ready), *in_hbm(w_down))


def halve_body(keep, arrived, low_here, low_there, high_here, high_there):
    total = keep[...] + arrived[...].astype(F32)
    rows, width = low_here.shape
    low_here[...] = total[:rows, :width]
    low_there[...] = total[:rows, width:]
    high_here[...] = total[rows:, :width].astype(BF16)
    high_there[...] = total[rows:, width:].astype(BF16)


def halve(keep, arrived):
    rows, width = keep.shape
    return pl.pallas_call(
        halve_body,
        in_specs=[VMEM] * 2,
        out_specs=[VMEM] * 4,
        out_shape=[jax.ShapeDtypeStruct((rows // 2, width // 2), t) for t in (F32, F32, BF16, BF16)],
        compiler_params=pltpu.CompilerParams(vmem_limit_bytes=SCOPE),
        name="halve",
    )(keep, arrived)


def deal_body(low, arrived, *outs):
    width = outs[0].shape[1]
    for i, out in enumerate(outs):
        s = slice(i * width, (i + 1) * width)
        out[...] = (low[:, s] + arrived[:, s].astype(F32)).astype(out.dtype)


def deal(low, arrived, kinds):
    rows, width = low.shape
    return pl.pallas_call(
        deal_body,
        in_specs=[VMEM] * 2,
        out_specs=[VMEM] * len(kinds),
        out_shape=[jax.ShapeDtypeStruct((rows, width // len(kinds)), t) for t in kinds],
        compiler_params=pltpu.CompilerParams(vmem_limit_bytes=SCOPE),
        name="deal",
    )(low, arrived)


def last_body(*refs):
    stream, parts, out = refs[0], refs[1:-1], refs[-1]
    total = parts[0][...]
    for part in parts[1:]:
        total = total + part[...].astype(F32)
    out[...] = (stream[...].astype(F32) + total).astype(BF16)


def last(stream, parts):
    return pl.pallas_call(
        last_body,
        in_specs=[VMEM] * (1 + len(parts)),
        out_specs=VMEM,
        out_shape=jax.ShapeDtypeStruct(stream.shape, BF16),
        compiler_params=pltpu.CompilerParams(vmem_limit_bytes=SCOPE),
        name="last",
    )(stream, *parts)


def shards_kernels(
    query,
    new_key,
    new_value,
    key_cache,
    value_cache,
    cache_len,
    resid,
    w_out,
    rms_gain,
    w_router,
    route_ids,
    w_gate,
    w_up,
    w_down,
):
    sides, tensors = lax.axis_size("side"), lax.axis_size("tensor")
    features = resid.shape[1]
    depth = query.shape[1]
    extra = features // sides // 2
    slots, _, hidden = w_gate.shape
    held = [1, 1, 1, 1, 1]
    weights = (w_gate, w_up, w_down)
    part = features // tensors
    block = 512 if part % 512 == 0 else LANES
    *blocks, w_here = attend(
        sides,
        extra,
        query,
        new_key,
        new_value,
        key_cache,
        value_cache,
        cache_len,
        resid,
        route_ids,
        w_out,
    )
    *more, block_0 = prefetch(0, held[0], weights, blocks[0], block, 0)
    ready = more
    blocks = [blocks[0]] + [swap(blocks[k], "side", sides, k) for k in range(1, sides)]
    mine, other = project(sides, blocks, w_here, ready[-1])
    ready += prefetch(len(ready), held[1], weights, other)
    mine, other = add(mine, swap(other, "tensor", tensors, 1), ready[-1])
    ready += prefetch(len(ready), held[2], weights, other)
    step = 2
    while step < tensors // 2:
        mine, other = add(mine, swap(other, "tensor", tensors, step), ready[-1])
        step *= 2
    stream = stream_of(sides, depth, mine, swap(other, "tensor", tensors, step), blocks, ready[-1])
    ready += prefetch(len(ready), held[3], weights, stream)
    own = join(stream, swap(stream, "tensor", tensors, 1), ready[-1])
    *more, block_1 = prefetch(len(ready), held[4], weights, own, block, 1)
    ready += more
    across = swap(own, "side", sides, 2)
    beside = swap(own, "side", sides, 1)
    across, block_1 = lax.optimization_barrier((across, block_1))
    chunks = [own, beside, across, swap(across, "side", sides, 1)]
    inner, mine = expand(
        sides,
        slots * sides // w_router.shape[1],
        chunks,
        blocks,
        rms_gain.reshape(1, features),
        w_router.T,
        w_gate,
        w_up,
        ready,
        part,
    )
    keep, send = contract(tensors, block, inner, [block_0, block_1], w_down)
    low_here, low_there, high_here, high_there = halve(keep, swap(send, "side", sides, 1))
    count = tensors // 2
    arrived = swap(high_there, "side", sides, 2)
    arrived, high_here = lax.optimization_barrier((arrived, high_here))
    there = deal(low_there, arrived, [BF16] * count)
    parts = [swap(v, "tensor", tensors, count + i) for i, v in enumerate(there)]
    kinds = [F32] + [BF16] * (count - 1)
    here = deal(low_here, swap(high_here, "side", sides, 2), kinds)
    parts += [swap(v, "tensor", tensors, i) for i, v in enumerate(here) if i]
    return last(mine, [here[0], *parts])


def attend_local(query, new_key, new_value, key_cache, value_cache, cache_len):
    count = query.shape[0]
    positions = key_cache.shape[1]
    kv_local = key_cache.shape[2] // HEAD_DIM
    repeat = query.shape[1] // (kv_local * HEAD_DIM)
    queries = query.reshape(count, kv_local, repeat, HEAD_DIM)
    cached_keys = key_cache.reshape(count, positions, kv_local, HEAD_DIM)
    cached_values = value_cache.reshape(count, positions, kv_local, HEAD_DIM)
    scale = 1.0 / HEAD_DIM**0.5
    scores = (
        jnp.einsum("gkrd,gpkd->gkrp", queries, cached_keys, preferred_element_type=jnp.float32)
        * scale
    )
    own_key = new_key.reshape(count, kv_local, HEAD_DIM)
    own_score = (
        jnp.einsum("gkrd,gkd->gkr", queries, own_key, preferred_element_type=jnp.float32) * scale
    )
    valid = jnp.arange(positions, dtype=jnp.int32)[None, :] < cache_len[:, None]
    scores = jnp.where(valid[:, None, None, :], scores, -jnp.inf)
    highest = jnp.maximum(jnp.max(scores, axis=-1), own_score)
    cached_weight = jnp.exp(scores - highest[..., None])
    own_weight = jnp.exp(own_score - highest)
    total = jnp.sum(cached_weight, axis=-1) + own_weight
    cached_weight = (cached_weight / total[..., None]).astype(jnp.bfloat16)
    own_weight = (own_weight / total).astype(jnp.bfloat16)
    mixed = jnp.einsum(
        "gkrp,gpkd->gkrd", cached_weight, cached_values, preferred_element_type=jnp.float32
    )
    own_value = new_value.reshape(count, kv_local, 1, HEAD_DIM).astype(jnp.float32)
    mixed = mixed + own_weight.astype(jnp.float32)[..., None] * own_value
    return mixed.reshape(count, kv_local * repeat * HEAD_DIM).astype(jnp.bfloat16)


def shards(
    query,
    new_key,
    new_value,
    key_cache,
    value_cache,
    cache_len,
    resid,
    w_out,
    rms_gain,
    w_router,
    route_ids,
    w_gate,
    w_up,
    w_down,
):
    attended = attend_local(query, new_key, new_value, key_cache, value_cache, cache_len)
    column_part = jnp.dot(
        lax.all_gather(attended, "side", axis=0, tiled=True),
        w_out,
        preferred_element_type=jnp.float32,
    )
    partial_out = lax.all_to_all(column_part, "side", split_axis=0, concat_axis=1, tiled=True)
    attn_out = lax.psum(partial_out, "tensor")
    stream = (resid.astype(jnp.float32) + attn_out).astype(jnp.bfloat16)
    wide = stream.astype(jnp.float32)
    power = jnp.mean(wide * wide, axis=-1, keepdims=True)
    normed = wide * lax.rsqrt(power + 1e-05) * rms_gain.astype(jnp.float32)
    logits = jnp.dot(normed, w_router, precision=lax.Precision.HIGHEST)
    experts = w_router.shape[1]
    picked = route_ids[:, :, None] == jnp.arange(experts, dtype=jnp.int32)[None, None, :]
    chosen = jnp.sum(jnp.where(picked, logits[:, None, :], 0.0), axis=-1)
    first = 1.0 / (1.0 + jnp.exp(chosen[:, 1] - chosen[:, 0]))
    second = 1.0 / (1.0 + jnp.exp(chosen[:, 0] - chosen[:, 1]))
    pair = jnp.stack([first, second], axis=1)
    weight = jnp.sum(jnp.where(picked, pair[:, :, None], 0.0), axis=1)
    rows = normed.astype(jnp.bfloat16)
    member = jnp.any(picked, axis=1).astype(jnp.int32)
    order_rank = jnp.cumsum(member, axis=0) - member
    capacity = CAP
    placing = (order_rank.T[:, None, :] == jnp.arange(capacity, dtype=jnp.int32)[None, :, None]) & (
        member.T[:, None, :] == 1
    )
    packed = jnp.einsum(
        "ecg,gd->ecd", placing.astype(jnp.bfloat16), rows, preferred_element_type=jnp.float32
    ).astype(jnp.bfloat16)
    side_count = lax.axis_size("side")
    slot_total = max(side_count, experts)
    split_count = slot_total // experts
    slot_local = slot_total // side_count
    width = rows.shape[1]
    packed = jnp.repeat(packed, split_count, axis=0).reshape(
        side_count, slot_local, capacity, width
    )
    arrived = lax.all_to_all(packed, "side", split_axis=0, concat_axis=0, tiled=True)
    gate = jnp.einsum("sjcd,jdf->sjcf", arrived, w_gate, preferred_element_type=jnp.float32)
    upward = jnp.einsum("sjcd,jdf->sjcf", arrived, w_up, preferred_element_type=jnp.float32)
    inner = (jax.nn.silu(gate) * upward).astype(jnp.bfloat16)
    expert_part = jnp.einsum("sjcf,jfd->sjcd", inner, w_down, preferred_element_type=jnp.float32)
    scaled_place = placing.astype(jnp.float32) * weight.T[:, None, :]
    returned = lax.all_to_all(expert_part, "side", split_axis=0, concat_axis=0, tiled=True)
    features = returned.shape[3]
    merged = jnp.sum(returned.reshape(experts, split_count, capacity, features), axis=1)
    moe = lax.psum_scatter(
        jnp.einsum("ecg,ecf->gf", scaled_place, merged, precision=lax.Precision.HIGHEST),
        "tensor",
        scatter_dimension=1,
        tiled=True,
    )
    columns = moe.shape[1]
    local_stream = lax.dynamic_slice_in_dim(wide, lax.axis_index("tensor") * columns, columns, 1)
    return (local_stream + moe).astype(jnp.bfloat16)


def tiles(mesh, sides=4):
    side, tensor = mesh.shape["side"], mesh.shape["tensor"]
    return side == sides and tensor >= 4 and tensor & (tensor - 1) == 0


def solution(mesh):
    return jax.shard_map(
        shards_kernels if tiles(mesh) else shards,
        mesh=mesh,
        in_specs=(
            P(("groups", "side"), "tensor"),
            P(("groups", "side"), "tensor"),
            P(("groups", "side"), "tensor"),
            P(("groups", "side"), None, "tensor"),
            P(("groups", "side"), None, "tensor"),
            P(("groups", "side")),
            P(("groups", "side"), None),
            P("tensor", "side"),
            P(),
            P(),
            P(("groups", "side"), None),
            P("side", None, "tensor"),
            P("side", None, "tensor"),
            P("side", "tensor", None),
        ),
        out_specs=P(("groups", "side"), "tensor"),
        check_vma=False,
    )
```

```python
import functools
import math

import jax
import jax.numpy as jnp
from jax import lax
from jax.experimental import pallas as pl
from jax.experimental.pallas import tpu as pltpu
from jax.sharding import PartitionSpec as P

HEAD_DIM = 128
CAP = 12
LANES = 128
FBLOCK = 256
BF16 = jnp.bfloat16
F32 = jnp.float32
SCOPE = 8 * 2**20
VMEM = pl.BlockSpec(memory_space=pltpu.VMEM)
ANY = pl.BlockSpec(memory_space=pl.ANY)
HBM = pl.BlockSpec(memory_space=pltpu.HBM)


def cost(flops, moved):
    return pl.CostEstimate(flops=int(flops), bytes_accessed=int(moved), transcendentals=0)


def place_of(position, count):
    bits = count.bit_length() - 1
    return sum(((position >> b) & 1) << (bits - 1 - b) for b in range(bits))


def swap(value, axis, count, mask):
    return lax.ppermute(value, axis, [(i, i ^ mask) for i in range(count)])


def in_hbm(*arrays):
    return [pltpu.with_memory_space_constraint(a, pltpu.HBM) for a in arrays]


def in_vmem(*arrays):
    return [pltpu.with_memory_space_constraint(a, pltpu.VMEM) for a in arrays]


def columns(start, size):
    return pl.ds(pl.multiple_of(start, LANES), size)


def attend_body(
    sides,
    block,
    length_at,
    query_at,
    new_key_at,
    new_value_at,
    keys_at,
    values_at,
    resid_at,
    route_at,
    w_out_at,
    *rest,
):
    outs, w_out, rest = rest[:sides], rest[sides], rest[sides + 1 :]
    query, new_key, new_value, keys, values, resid, route, sems, rest = *rest[:8], rest[8:]
    length, spread, mixed, score, own_score, key32, value32 = rest
    games, width = query.shape
    heads = width // HEAD_DIM
    padded = spread.shape[1]
    wide = new_key.shape[1]
    repeat = heads * HEAD_DIM // wide
    scale = 1.0 / HEAD_DIM**0.5
    steps = games // block

    def copy(source, target, sem):
        return pltpu.make_async_copy(source, target, sems.at[sem])

    small = [
        copy(source, target, i)
        for i, (source, target) in enumerate(
            (
                (query_at, query),
                (new_key_at, new_key),
                (new_value_at, new_value),
                (route_at, route),
                (resid_at, resid),
            )
        )
    ]
    caches = [
        [
            copy(source.at[pl.ds(i * block, block)], target.at[pl.ds(i * block, block)], sem + i)
            for i in range(steps)
        ]
        for source, target, sem in ((keys_at, keys, 5), (values_at, values, 5 + steps))
    ]
    after = copy(w_out_at, w_out, 5 + 2 * steps)
    lengths = copy(length_at, length, 6 + 2 * steps)
    for c in [lengths] + small[:4] + caches[0] + caches[1] + small[4:] + [after]:
        c.start()
    spread[...] = jnp.zeros_like(spread)
    for c in [lengths] + small[:4]:
        c.wait()
    for h in range(heads):
        lane = h // repeat * HEAD_DIM
        spread[:, h, lane : lane + HEAD_DIM] = query[
            :, h * HEAD_DIM : (h + 1) * HEAD_DIM
        ].astype(F32)
    key32[...] = new_key[...].astype(F32)
    value32[...] = new_value[...].astype(F32)
    for game in range(games):
        if game % block == 0:
            caches[0][game // block].wait()
        q = spread[game]
        s = slice(game * padded, (game + 1) * padded)
        value = (
            lax.dot_general(
                q.astype(BF16), keys[game], (((1,), (1,)), ((), ())), preferred_element_type=F32
            )
            * scale
        )
        at = lax.broadcasted_iota(jnp.int32, value.shape, 1)
        score[s] = jnp.where(at < length[game], value, -jnp.inf)
        own = jnp.sum(q * key32[game : game + 1, :], axis=-1, keepdims=True) * scale
        own_score[s] = jnp.broadcast_to(own, (padded, LANES))
    for i in range(steps):
        s = slice(i * block * padded, (i + 1) * block * padded)
        own = own_score[s][:, :1]
        value = score[s]
        top = jnp.maximum(jnp.max(value, axis=-1, keepdims=True), own)
        e = jnp.exp(value - top)
        own_e = jnp.exp(own - top)
        total = jnp.sum(e, axis=-1, keepdims=True) + own_e
        score[s] = e / total
        own_score[s] = jnp.broadcast_to(
            (own_e / total).astype(BF16).astype(F32), (block * padded, LANES)
        )
        caches[1][i].wait()
        for game in range(i * block, (i + 1) * block):
            s = slice(game * padded, (game + 1) * padded)
            mixed[game] = (
                jnp.dot(score[s].astype(BF16), values[game], preferred_element_type=F32)
                + own_score[s][:, :1] * value32[game : game + 1, :]
            )
    small[4].wait()
    side, tensor = lax.axis_index("side"), lax.axis_index("tensor")
    for h in range(heads):
        lane = h // repeat * HEAD_DIM
        part = mixed[:, h, lane : lane + HEAD_DIM].astype(BF16)
        for out in outs:
            out[:, h * HEAD_DIM : (h + 1) * HEAD_DIM] = part
    extra = outs[0].shape[1] - width - LANES
    row = lax.broadcasted_iota(jnp.int32, (games, games), 0)
    diagonal = row == lax.broadcasted_iota(jnp.int32, (games, games), 1)
    lane = lax.broadcasted_iota(jnp.int32, (games, LANES), 1)
    routes = jnp.zeros((games, LANES), F32)
    for j in range(route.shape[0]):
        ids = jnp.broadcast_to(route[j : j + 1, :].astype(F32), (games, games))
        column = jnp.sum(jnp.where(diagonal, ids, 0.0), axis=-1, keepdims=True)
        routes = jnp.where(lane == j, column, routes)
    features = resid.shape[1] // sides
    for k, out in enumerate(outs):
        start = jnp.bitwise_xor(side, k) * features + tensor % 2 * extra
        out[:, width : width + extra] = resid[:, columns(start, extra)]
        out[:, width + extra :] = routes.astype(BF16)
    after.wait()


def attend(
    sides, extra, query, new_key, new_value, key_cache, value_cache, cache_len, resid, route_ids, w_out
):
    games, width = query.shape
    positions, wide = key_cache.shape[1:]
    block = 4
    heads = -(-(width // HEAD_DIM) // 16) * 16
    out = jax.ShapeDtypeStruct((games, width + extra + LANES), BF16)
    routes = route_ids.T
    arrays = [query, new_key, new_value, key_cache, value_cache, resid, routes]
    return pl.pallas_call(
        functools.partial(attend_body, sides, block),
        in_specs=[HBM] * (len(arrays) + 2),
        out_specs=[VMEM] * (sides + 1),
        out_shape=[out] * sides + [pltpu.VMEM(w_out.shape, BF16)],
        scratch_shapes=[pltpu.VMEM(a.shape, a.dtype) for a in arrays]
        + [
            pltpu.SemaphoreType.DMA((7 + 2 * (games // block),)),
            pltpu.SMEM(cache_len.shape, jnp.int32),
            pltpu.VMEM((games, heads, wide), F32),
            pltpu.VMEM((games, heads, wide), F32),
            pltpu.VMEM((games * heads, positions), F32),
            pltpu.VMEM((games * heads, LANES), F32),
            pltpu.VMEM((games, wide), F32),
            pltpu.VMEM((games, wide), F32),
        ],
        compiler_params=pltpu.CompilerParams(vmem_limit_bytes=SCOPE),
        cost_estimate=cost(4 * games * heads * positions * wide, 2 * key_cache.size * 2),
        name="attend",
    )(*in_hbm(cache_len, *arrays, w_out))


def project_body(sides, *refs):
    blocks, weight = refs[:sides], refs[sides]
    mine, other, rows, total = refs[sides + 2 :]
    games = blocks[0].shape[0]
    depth, width = weight.shape
    for p in range(sides):
        rows[p * games : (p + 1) * games, :] = blocks[place_of(p, sides)][:, :depth]
    step = 512 if width % 512 == 0 else LANES
    for c in range(0, width, step):
        total[:, c : c + step] = jnp.dot(
            rows[...], weight[:, c : c + step], preferred_element_type=F32
        )
    odd = lax.axis_index("tensor") % 2
    half = width // 2
    mine[...] = total[:, columns(odd * half, half)]
    other[...] = total[:, columns((1 - odd) * half, half)].astype(BF16)


def project(sides, blocks, w_out, after):
    rows = blocks[0].shape[0] * sides
    depth, width = w_out.shape
    return pl.pallas_call(
        functools.partial(project_body, sides),
        in_specs=[VMEM] * (sides + 2),
        out_specs=[VMEM] * 2,
        out_shape=[
            jax.ShapeDtypeStruct((rows, width // 2), F32),
            jax.ShapeDtypeStruct((rows, width // 2), BF16),
        ],
        scratch_shapes=[pltpu.VMEM((rows, depth), BF16), pltpu.VMEM((rows, width), F32)],
        compiler_params=pltpu.CompilerParams(vmem_limit_bytes=SCOPE),
        cost_estimate=cost(2 * rows * depth * width, 2 * depth * width),
        name="project",
    )(*blocks, *in_vmem(w_out, after))


def add_body(mine, arrived, after, total, rounded):
    del after
    value = mine[...] + arrived[...].astype(F32)
    total[...] = value
    rounded[...] = value.astype(BF16)


def add(mine, arrived, after):
    return pl.pallas_call(
        add_body,
        in_specs=[VMEM, VMEM, VMEM],
        out_specs=[VMEM] * 2,
        out_shape=[
            jax.ShapeDtypeStruct(mine.shape, F32),
            jax.ShapeDtypeStruct(mine.shape, BF16),
        ],
        compiler_params=pltpu.CompilerParams(vmem_limit_bytes=SCOPE),
        name="add",
    )(mine, arrived, *in_vmem(after))


def stream_body(sides, depth, mine, arrived, *refs):
    blocks, out = refs[:sides], refs[-1]
    games = blocks[0].shape[0]
    width = out.shape[1]
    for p in range(sides):
        s = slice(p * games, (p + 1) * games)
        resid = blocks[place_of(p, sides)][:, depth : depth + width].astype(F32)
        out[s, :] = (resid + (mine[s] + arrived[s].astype(F32))).astype(BF16)


def stream_of(sides, depth, mine, arrived, blocks, after):
    return pl.pallas_call(
        functools.partial(stream_body, sides, depth),
        in_specs=[VMEM] * (sides + 3),
        out_specs=VMEM,
        out_shape=jax.ShapeDtypeStruct(mine.shape, BF16),
        compiler_params=pltpu.CompilerParams(vmem_limit_bytes=SCOPE),
        name="stream",
    )(mine, arrived, *blocks, *in_vmem(after))


def join_body(mine, arrived, after, out):
    del after
    width = mine.shape[1]
    odd = lax.axis_index("tensor") % 2
    out[:, columns(odd * width, width)] = mine[...]
    out[:, columns((1 - odd) * width, width)] = arrived[...]


def join(mine, arrived, after):
    rows, width = mine.shape
    return pl.pallas_call(
        join_body,
        in_specs=[VMEM] * 3,
        out_specs=VMEM,
        out_shape=jax.ShapeDtypeStruct((rows, 2 * width), BF16),
        compiler_params=pltpu.CompilerParams(vmem_limit_bytes=SCOPE),
        name="join",
    )(mine, arrived, *in_vmem(after))


def prefetch_body(first, count, per_slot, block, number, w_gate, w_up, w_down, after, *refs):
    del after
    outs, sems = refs[:-1], refs[-1]
    copies = []
    if block:
        start = lax.axis_index("tensor") * (w_down.shape[2] // lax.axis_size("tensor"))
        start = start + number * block
        for i in range(w_down.shape[0]):
            copies.append(
                pltpu.make_async_copy(
                    w_down.at[i, :, columns(start, block)],
                    outs[count].at[pl.ds(i * w_down.shape[1], w_down.shape[1])],
                    sems.at[count, i],
                )
            )
    for i, out in enumerate(outs[:count]):
        slot, block = divmod(first + i, per_slot)
        for half, weight in enumerate((w_gate, w_up)):
            copies.append(
                pltpu.make_async_copy(
                    weight.at[slot, :, pl.ds(block * FBLOCK, FBLOCK)],
                    out.at[half],
                    sems.at[i, half],
                )
            )
    for c in copies:
        c.start()
    for c in copies:
        c.wait()


def prefetch(first, count, weights, after, block=0, number=0):
    w_gate, _, w_down = weights
    slots, depth, hidden = w_gate.shape
    shapes = [(2, depth, FBLOCK)] * count + [(slots * hidden, block)] * bool(block)
    return list(
        pl.pallas_call(
            functools.partial(prefetch_body, first, count, hidden // FBLOCK, block, number),
            in_specs=[HBM] * 3 + [VMEM],
            out_specs=[VMEM] * len(shapes),
            out_shape=[pltpu.VMEM(s, BF16) for s in shapes],
            scratch_shapes=[pltpu.SemaphoreType.DMA((len(shapes), max(2, slots)))],
            compiler_params=pltpu.CompilerParams(vmem_limit_bytes=SCOPE),
            cost_estimate=cost(0, sum(2 * math.prod(s) for s in shapes)),
            name="prefetch",
        )(*in_hbm(*weights), after)
    )


def halves(value, gain, rows, where):
    count = value.shape[0]
    scaled = value.astype(F32) * gain.astype(F32)
    high = scaled.astype(BF16)
    rows[:count, where] = high
    rows[count:, where] = (scaled - high.astype(F32)).astype(BF16)


def fold(value):
    count = value.shape[0] // 2
    return value[:count] + value[count:]


def expand_body(sides, kept, split, ring, *refs):
    chunks, refs = refs[:sides], refs[sides:]
    blocks, refs = refs[:sides], refs[sides:]
    gain, router, w_gate, w_up = refs[:4]
    ready, refs = refs[4 : 4 + kept], refs[4 + kept :]
    inner, mine, stream, rows, router2, scale, norms, raw, buffer, sems = refs
    games = blocks[0].shape[0]
    count = games * sides
    width = chunks[0].shape[1]
    features = width * sides
    slots, _, hidden = w_gate.shape
    per_slot = hidden // FBLOCK
    streamed = slots * per_slot - kept
    side, tensor = lax.axis_index("side"), lax.axis_index("tensor")

    def copies(step):
        index = kept + step
        return [
            pltpu.make_async_copy(
                weight.at[index // per_slot, :, columns(index % per_slot * FBLOCK, FBLOCK)],
                buffer.at[step % ring, half],
                sems.at[step % ring, half],
            )
            for half, weight in enumerate((w_gate, w_up))
        ]

    for step in range(min(ring, streamed)):
        for c in copies(step):
            c.start()

    power = jnp.zeros((count, LANES), F32)
    experts = router.shape[0]
    for k in range(sides):
        base = jnp.bitwise_xor(side, k) * width
        flip = place_of(k, sides)
        for c in range(0, width, 512):
            value = jnp.concatenate(
                [
                    chunks[k][(p ^ flip) * games : (p ^ flip) * games + games, c : c + 512]
                    for p in range(sides)
                ],
                axis=0,
            )
            wide = value.astype(F32)
            for i in range(0, 512, LANES):
                power = power + wide[:, i : i + LANES] * wide[:, i : i + LANES]
            there = columns(base + c, 512)
            stream[:, there] = value[:games]
            halves(value, gain[:, there], rows, there)
            weight = router[:, there]
            top = weight.astype(BF16).astype(F32)
            router2[:, there] = jnp.concatenate([top, weight - top], axis=0).astype(BF16)
    norm = lax.rsqrt(jnp.sum(power, axis=-1, keepdims=True) / features + 1e-05)
    norms[...] = jnp.broadcast_to(norm, norms.shape)
    products = fold(
        lax.dot_general(
            rows[...], router2[...], (((1,), (1,)), ((), ())), preferred_element_type=F32
        )
    )
    logits = (products[:, :experts] + products[:, experts:]) * norm
    route = jnp.concatenate(
        [blocks[place_of(p, sides)][:, -LANES:] for p in range(sides)], axis=0
    ).astype(F32)
    lane = lax.broadcasted_iota(jnp.int32, route.shape, 1)
    ids = [jnp.sum(jnp.where(lane == j, route, 0.0), axis=-1, keepdims=True) for j in range(2)]
    number = lax.broadcasted_iota(jnp.int32, logits.shape, 1).astype(F32)
    chosen = [
        jnp.sum(jnp.where(number == ids[j], logits, 0.0), axis=-1, keepdims=True)
        for j in range(2)
    ]
    shares = [
        1.0 / (1.0 + jnp.exp(chosen[1] - chosen[0])),
        1.0 / (1.0 + jnp.exp(chosen[0] - chosen[1])),
    ]
    for i in range(slots):
        expert = ((side * slots + i) // split).astype(F32)
        weight = jnp.where(ids[0] == expert, shares[0], 0.0) + jnp.where(
            ids[1] == expert, shares[1], 0.0
        )
        scale[i] = jnp.broadcast_to(weight, (count, FBLOCK))
    mine[...] = stream[:, columns(tensor * mine.shape[1], mine.shape[1])]

    def products(weights, turn):
        for half in range(2):
            raw[turn % 2, half] = fold(
                jnp.dot(rows[...], weights[half], preferred_element_type=F32)
            )

    def finish(index, turn):
        gate = raw[turn % 2, 0] * norms[...]
        upward = raw[turn % 2, 1] * norms[...]
        value = gate / (1.0 + jnp.exp(-gate)) * upward * scale[index // per_slot]
        where = columns(index * FBLOCK, FBLOCK)
        high = value.astype(BF16)
        inner[:count, where] = high
        inner[count:, where] = (value - high.astype(F32)).astype(BF16)

    def from_ring(step, turn, before):
        for c in copies(step):
            c.wait()
        products(buffer.at[step % ring], turn)
        if before is not None:
            finish(before, turn + 1)

        @pl.when(step + ring < streamed)
        def _():
            for c in copies(step + ring):
                c.start()

    done, before = 0, None
    for index in range(kept + 1):
        until = streamed * (index + 1) // (kept + 1)
        if done < until:
            from_ring(jnp.int32(done), done + index, before)

            @pl.loop(done + 1, until)
            def _(step):
                from_ring(step, step + index, kept + step - 1)

            done, before = until, kept + until - 1
        if index < kept:
            products(ready[index], done + index)
            if before is not None:
                finish(before, done + index + 1)
            before = index
    finish(before, streamed + kept - 1)


def expand(sides, split, chunks, blocks, gain, router, w_gate, w_up, ready, own_width):
    games = blocks[0].shape[0]
    count = games * sides
    features = chunks[0].shape[1] * sides
    slots, _, hidden = w_gate.shape
    ring = 2
    arguments = [*chunks, *blocks, gain, router]
    return pl.pallas_call(
        functools.partial(expand_body, sides, len(ready), split, ring),
        in_specs=[VMEM] * len(arguments) + [HBM] * 2 + [VMEM] * len(ready),
        out_specs=[VMEM] * 2,
        out_shape=[
            jax.ShapeDtypeStruct((2 * count, slots * hidden), BF16),
            jax.ShapeDtypeStruct((games, own_width), BF16),
        ],
        scratch_shapes=[
            pltpu.VMEM((games, features), BF16),
            pltpu.VMEM((2 * count, features), BF16),
            pltpu.VMEM((2 * router.shape[0], features), BF16),
            pltpu.VMEM((slots, count, FBLOCK), F32),
            pltpu.VMEM((count, FBLOCK), F32),
            pltpu.VMEM((2, 2, count, FBLOCK), F32),
            pltpu.VMEM((ring, 2, features, FBLOCK), BF16),
            pltpu.SemaphoreType.DMA((ring, 2)),
        ],
        compiler_params=pltpu.CompilerParams(vmem_limit_bytes=16 * 2**20),
        cost_estimate=cost(8 * count * w_gate.size, 2 * w_gate.size * 2),
        name="expand",
    )(*arguments, *in_hbm(w_gate, w_up), *in_vmem(*ready))


def contract_body(tensors, ring, block, kept, inner, *refs):
    ready, (w_down, keep, send, buffer, sems) = refs[:kept], refs[kept:]
    slots, hidden, features = w_down.shape
    tensor = lax.axis_index("tensor")
    part = features // tensors
    per_part = part // block
    steps = features // block
    half = keep.shape[0]
    deep = ring // slots

    def copies(step):
        start = jnp.bitwise_xor(tensor, step // per_part) * part + step % per_part * block
        return [
            pltpu.make_async_copy(
                w_down.at[slot, :, columns(start, block)],
                buffer.at[step % deep, pl.ds(slot * hidden, hidden)],
                sems.at[step % deep, slot],
            )
            for slot in range(slots)
        ]

    for step in range(kept, min(deep + kept, steps)):
        for c in copies(step):
            c.start()

    def run(step, more, weights, arriving=()):
        for c in arriving:
            c.wait()
        total = fold(jnp.dot(inner[...], weights[...], preferred_element_type=F32))
        where = columns(step * block, block)
        keep[:, where] = total[:half]
        send[:, where] = total[half:].astype(BF16)
        if more:
            for c in copies(step + deep):
                c.start()

    def from_ring(step, more):
        run(step, more, buffer.at[step % deep], copies(step))

    for step, weights in enumerate(ready):
        run(step, False, weights)
    edge = max(kept, steps - deep)
    pl.loop(kept, edge)(lambda step: from_ring(step, True))
    for step in range(edge, steps):
        from_ring(step, False)


def contract(tensors, block, inner, ready, w_down):
    count = inner.shape[0] // 2
    slots, hidden, features = w_down.shape
    ring = 3 * slots
    return pl.pallas_call(
        functools.partial(contract_body, tensors, ring, block, len(ready)),
        in_specs=[VMEM] * (1 + len(ready)) + [HBM],
        out_specs=[VMEM, VMEM],
        out_shape=[
            jax.ShapeDtypeStruct((count // 2, features), F32),
            jax.ShapeDtypeStruct((count // 2, features), BF16),
        ],
        scratch_shapes=[
            pltpu.VMEM((ring // slots, slots * hidden, block), BF16),
            pltpu.SemaphoreType.DMA((ring // slots, slots)),
        ],
        compiler_params=pltpu.CompilerParams(vmem_limit_bytes=16 * 2**20),
        cost_estimate=cost(4 * count * w_down.size, 2 * w_down.size),
        name="contract",
    )(inner, *in_vmem(*ready), *in_hbm(w_down))


def halve_body(keep, arrived, low_here, low_there, high_here, high_there):
    total = keep[...] + arrived[...].astype(F32)
    rows, width = low_here.shape
    low_here[...] = total[:rows, :width]
    low_there[...] = total[:rows, width:]
    high_here[...] = total[rows:, :width].astype(BF16)
    high_there[...] = total[rows:, width:].astype(BF16)


def halve(keep, arrived):
    rows, width = keep.shape
    return pl.pallas_call(
        halve_body,
        in_specs=[VMEM] * 2,
        out_specs=[VMEM] * 4,
        out_shape=[jax.ShapeDtypeStruct((rows // 2, width // 2), t) for t in (F32, F32, BF16, BF16)],
        compiler_params=pltpu.CompilerParams(vmem_limit_bytes=SCOPE),
        name="halve",
    )(keep, arrived)


def deal_body(low, arrived, *outs):
    width = outs[0].shape[1]
    for i, out in enumerate(outs):
        s = slice(i * width, (i + 1) * width)
        out[...] = (low[:, s] + arrived[:, s].astype(F32)).astype(out.dtype)


def deal(low, arrived, kinds):
    rows, width = low.shape
    return pl.pallas_call(
        deal_body,
        in_specs=[VMEM] * 2,
        out_specs=[VMEM] * len(kinds),
        out_shape=[jax.ShapeDtypeStruct((rows, width // len(kinds)), t) for t in kinds],
        compiler_params=pltpu.CompilerParams(vmem_limit_bytes=SCOPE),
        name="deal",
    )(low, arrived)


def last_body(*refs):
    stream, parts, out = refs[0], refs[1:-1], refs[-1]
    total = parts[0][...]
    for part in parts[1:]:
        total = total + part[...].astype(F32)
    out[...] = (stream[...].astype(F32) + total).astype(BF16)


def last(stream, parts):
    return pl.pallas_call(
        last_body,
        in_specs=[VMEM] * (1 + len(parts)),
        out_specs=VMEM,
        out_shape=jax.ShapeDtypeStruct(stream.shape, BF16),
        compiler_params=pltpu.CompilerParams(vmem_limit_bytes=SCOPE),
        name="last",
    )(stream, *parts)


def shards_kernels(
    query,
    new_key,
    new_value,
    key_cache,
    value_cache,
    cache_len,
    resid,
    w_out,
    rms_gain,
    w_router,
    route_ids,
    w_gate,
    w_up,
    w_down,
):
    sides, tensors = lax.axis_size("side"), lax.axis_size("tensor")
    features = resid.shape[1]
    depth = query.shape[1]
    extra = features // sides // 2
    slots, _, hidden = w_gate.shape
    held = [1, 1, 1, 1, 1]
    weights = (w_gate, w_up, w_down)
    part = features // tensors
    block = 512 if part % 512 == 0 else LANES
    *blocks, w_here = attend(
        sides,
        extra,
        query,
        new_key,
        new_value,
        key_cache,
        value_cache,
        cache_len,
        resid,
        route_ids,
        w_out,
    )
    *more, block_0 = prefetch(0, held[0], weights, blocks[0], block, 0)
    ready = more
    blocks = [blocks[0]] + [swap(blocks[k], "side", sides, k) for k in range(1, sides)]
    mine, other = project(sides, blocks, w_here, ready[-1])
    ready += prefetch(len(ready), held[1], weights, other)
    mine, other = add(mine, swap(other, "tensor", tensors, 1), ready[-1])
    ready += prefetch(len(ready), held[2], weights, other)
    step = 2
    while step < tensors // 2:
        mine, other = add(mine, swap(other, "tensor", tensors, step), ready[-1])
        step *= 2
    stream = stream_of(sides, depth, mine, swap(other, "tensor", tensors, step), blocks, ready[-1])
    ready += prefetch(len(ready), held[3], weights, stream)
    own = join(stream, swap(stream, "tensor", tensors, 1), ready[-1])
    *more, block_1 = prefetch(len(ready), held[4], weights, own, block, 1)
    ready += more
    across = swap(own, "side", sides, 2)
    beside = swap(own, "side", sides, 1)
    across, block_1 = lax.optimization_barrier((across, block_1))
    chunks = [own, beside, across, swap(across, "side", sides, 1)]
    inner, mine = expand(
        sides,
        slots * sides // w_router.shape[1],
        chunks,
        blocks,
        rms_gain.reshape(1, features),
        w_router.T,
        w_gate,
        w_up,
        ready,
        part,
    )
    keep, send = contract(tensors, block, inner, [block_0, block_1], w_down)
    low_here, low_there, high_here, high_there = halve(keep, swap(send, "side", sides, 1))
    count = tensors // 2
    arrived = swap(high_there, "side", sides, 2)
    arrived, high_here = lax.optimization_barrier((arrived, high_here))
    there = deal(low_there, arrived, [BF16] * count)
    parts = [swap(v, "tensor", tensors, count + i) for i, v in enumerate(there)]
    kinds = [F32] + [BF16] * (count - 1)
    here = deal(low_here, swap(high_here, "side", sides, 2), kinds)
    parts += [swap(v, "tensor", tensors, i) for i, v in enumerate(here) if i]
    return last(mine, [here[0], *parts])


def attend_local(query, new_key, new_value, key_cache, value_cache, cache_len):
    count = query.shape[0]
    positions = key_cache.shape[1]
    kv_local = key_cache.shape[2] // HEAD_DIM
    repeat = query.shape[1] // (kv_local * HEAD_DIM)
    queries = query.reshape(count, kv_local, repeat, HEAD_DIM)
    cached_keys = key_cache.reshape(count, positions, kv_local, HEAD_DIM)
    cached_values = value_cache.reshape(count, positions, kv_local, HEAD_DIM)
    scale = 1.0 / HEAD_DIM**0.5
    scores = (
        jnp.einsum("gkrd,gpkd->gkrp", queries, cached_keys, preferred_element_type=jnp.float32)
        * scale
    )
    own_key = new_key.reshape(count, kv_local, HEAD_DIM)
    own_score = (
        jnp.einsum("gkrd,gkd->gkr", queries, own_key, preferred_element_type=jnp.float32) * scale
    )
    valid = jnp.arange(positions, dtype=jnp.int32)[None, :] < cache_len[:, None]
    scores = jnp.where(valid[:, None, None, :], scores, -jnp.inf)
    highest = jnp.maximum(jnp.max(scores, axis=-1), own_score)
    cached_weight = jnp.exp(scores - highest[..., None])
    own_weight = jnp.exp(own_score - highest)
    total = jnp.sum(cached_weight, axis=-1) + own_weight
    cached_weight = (cached_weight / total[..., None]).astype(jnp.bfloat16)
    own_weight = (own_weight / total).astype(jnp.bfloat16)
    mixed = jnp.einsum(
        "gkrp,gpkd->gkrd", cached_weight, cached_values, preferred_element_type=jnp.float32
    )
    own_value = new_value.reshape(count, kv_local, 1, HEAD_DIM).astype(jnp.float32)
    mixed = mixed + own_weight.astype(jnp.float32)[..., None] * own_value
    return mixed.reshape(count, kv_local * repeat * HEAD_DIM).astype(jnp.bfloat16)


def shards(
    query,
    new_key,
    new_value,
    key_cache,
    value_cache,
    cache_len,
    resid,
    w_out,
    rms_gain,
    w_router,
    route_ids,
    w_gate,
    w_up,
    w_down,
):
    attended = attend_local(query, new_key, new_value, key_cache, value_cache, cache_len)
    column_part = jnp.dot(
        lax.all_gather(attended, "side", axis=0, tiled=True),
        w_out,
        preferred_element_type=jnp.float32,
    )
    partial_out = lax.all_to_all(column_part, "side", split_axis=0, concat_axis=1, tiled=True)
    attn_out = lax.psum(partial_out, "tensor")
    stream = (resid.astype(jnp.float32) + attn_out).astype(jnp.bfloat16)
    wide = stream.astype(jnp.float32)
    power = jnp.mean(wide * wide, axis=-1, keepdims=True)
    normed = wide * lax.rsqrt(power + 1e-05) * rms_gain.astype(jnp.float32)
    logits = jnp.dot(normed, w_router, precision=lax.Precision.HIGHEST)
    experts = w_router.shape[1]
    picked = route_ids[:, :, None] == jnp.arange(experts, dtype=jnp.int32)[None, None, :]
    chosen = jnp.sum(jnp.where(picked, logits[:, None, :], 0.0), axis=-1)
    first = 1.0 / (1.0 + jnp.exp(chosen[:, 1] - chosen[:, 0]))
    second = 1.0 / (1.0 + jnp.exp(chosen[:, 0] - chosen[:, 1]))
    pair = jnp.stack([first, second], axis=1)
    weight = jnp.sum(jnp.where(picked, pair[:, :, None], 0.0), axis=1)
    rows = normed.astype(jnp.bfloat16)
    member = jnp.any(picked, axis=1).astype(jnp.int32)
    order_rank = jnp.cumsum(member, axis=0) - member
    capacity = CAP
    placing = (order_rank.T[:, None, :] == jnp.arange(capacity, dtype=jnp.int32)[None, :, None]) & (
        member.T[:, None, :] == 1
    )
    packed = jnp.einsum(
        "ecg,gd->ecd", placing.astype(jnp.bfloat16), rows, preferred_element_type=jnp.float32
    ).astype(jnp.bfloat16)
    side_count = lax.axis_size("side")
    slot_total = max(side_count, experts)
    split_count = slot_total // experts
    slot_local = slot_total // side_count
    width = rows.shape[1]
    packed = jnp.repeat(packed, split_count, axis=0).reshape(
        side_count, slot_local, capacity, width
    )
    arrived = lax.all_to_all(packed, "side", split_axis=0, concat_axis=0, tiled=True)
    gate = jnp.einsum("sjcd,jdf->sjcf", arrived, w_gate, preferred_element_type=jnp.float32)
    upward = jnp.einsum("sjcd,jdf->sjcf", arrived, w_up, preferred_element_type=jnp.float32)
    inner = (jax.nn.silu(gate) * upward).astype(jnp.bfloat16)
    expert_part = jnp.einsum("sjcf,jfd->sjcd", inner, w_down, preferred_element_type=jnp.float32)
    scaled_place = placing.astype(jnp.float32) * weight.T[:, None, :]
    returned = lax.all_to_all(expert_part, "side", split_axis=0, concat_axis=0, tiled=True)
    features = returned.shape[3]
    merged = jnp.sum(returned.reshape(experts, split_count, capacity, features), axis=1)
    moe = lax.psum_scatter(
        jnp.einsum("ecg,ecf->gf", scaled_place, merged, precision=lax.Precision.HIGHEST),
        "tensor",
        scatter_dimension=1,
        tiled=True,
    )
    columns = moe.shape[1]
    local_stream = lax.dynamic_slice_in_dim(wide, lax.axis_index("tensor") * columns, columns, 1)
    return (local_stream + moe).astype(jnp.bfloat16)


def tiles(mesh, sides=4):
    side, tensor = mesh.shape["side"], mesh.shape["tensor"]
    return side == sides and tensor >= 4 and tensor & (tensor - 1) == 0


def solution(mesh):
    return jax.shard_map(
        shards_kernels if tiles(mesh) else shards,
        mesh=mesh,
        in_specs=(
            P(("groups", "side"), "tensor"),
            P(("groups", "side"), "tensor"),
            P(("groups", "side"), "tensor"),
            P(("groups", "side"), None, "tensor"),
            P(("groups", "side"), None, "tensor"),
            P(("groups", "side")),
            P(("groups", "side"), None),
            P("tensor", "side"),
            P(),
            P(),
            P(("groups", "side"), None),
            P("side", None, "tensor"),
            P("side", None, "tensor"),
            P("side", "tensor", None),
        ),
        out_specs=P(("groups", "side"), "tensor"),
        check_vma=False,
    )
```
